512 devices in a mesh: date: 16 (over x, z_hi), line: 32 (over z_lo, y, core).
Axes of the slice: x: 4, y: 4, z: 16 (z_hi: 4, z_lo: 4; z = z_hi * 4 + z_lo), core: 2. Of those that a mesh axis runs over, the one named last changes fastest.
Arguments:
- reference_slc: float32 [2, 384, 12288], P(None, 'line', 'date'), may hold values from -6 to 6
- secondary_slc: float32 [16, 2, 384, 12288], P('date', None, 'line'), may hold values from -6 to 6
- range_start: int32 [16], P('date'), may hold values from 0 to 12287
- azimuth_start: int32 [16], P('date'), may hold values from 0 to 383
Outputs:
- interferogram: float32 [16, 2, 384, 12288], P('date', None, 'line')
The draws below stay inside these ranges and needn't reach their ends.
All inputs are finite; a program needn't handle non-finite values.
Results may differ from the reference program's by a relative error of at most 0.0003.
Values sent between devices are 32-bit elements; how exact they have to be, the bound alone decides.
A program may use at most 128 MiB of HBM per device.

```python
import jax
import jax.numpy as jnp
from jax import lax

RG = 12288
RBAND = 8192
AZ = 384
ABAND = 192
DATES = 16


def touch_ends(entries, rng, smallest, top_value):
    index_at = [jax.random.randint(jax.random.fold_in(rng, axis), (), 0, length) for axis, length in enumerate(entries.shape)]
    widest = entries.shape.index(max(entries.shape))
    next_to = index_at[:widest] + [(index_at[widest] + 1) % entries.shape[widest]] + index_at[widest + 1:]
    return entries.at[tuple(index_at)].set(smallest).at[tuple(next_to)].set(top_value)


def levels(rng, dims, pieces, least, high):
    gain, own = 1.0, jax.random.fold_in(rng, 6)
    for dim, parts in pieces:
        heights = jnp.exp(jax.random.uniform(jax.random.fold_in(own, dim), (parts,), jnp.float32, least / len(pieces), high / len(pieces)))
        gain = gain * jnp.repeat(heights, dims[dim] // parts).reshape([-1 if axis == dim else 1 for axis in range(len(dims))])
    return gain


def normal_values(own_key, dims, width, bound, split=(), kind=jnp.bfloat16):
    values = width * jax.random.normal(own_key, dims, jnp.float32)
    if split:
        values = values * levels(own_key, dims, split, -0.22, 0.18)
    return jnp.clip(values, -bound, bound).astype(kind)


def setup_inputs(seed: int = 0) -> dict:
    splits = jax.random.split(jax.random.key(seed), 5)
    return {
        "reference_slc": normal_values(splits[0], (2, AZ, RG), 1.0, 6.0, ((1, 32), (2, 16)), jnp.float32),
        "secondary_slc": normal_values(splits[1], (DATES, 2, AZ, RG), 1.0, 6.0, ((0, 16), (2, 32)), jnp.float32),
        "range_start": touch_ends(jax.random.randint(splits[2], (DATES,), 0, RG), jax.random.fold_in(splits[2], 1), 0, RG - 1).astype(jnp.int32),
        "azimuth_start": touch_ends(jax.random.randint(splits[3], (DATES,), 0, AZ), jax.random.fold_in(splits[3], 1), 0, AZ - 1).astype(jnp.int32),
    }


def reference(reference_slc, secondary_slc, range_start, azimuth_start):
    ref_spectrum = jnp.fft.fft2(lax.complex(reference_slc[0], reference_slc[1]))
    range_bins = jnp.arange(RG, dtype=jnp.int32)
    doppler_bins = jnp.arange(AZ, dtype=jnp.int32)

    def one_date(packed):
        secondary, range_first, doppler_first = packed
        range_keep = (((range_bins - range_first) % RG) < RBAND).astype(jnp.float32)
        doppler_keep = (((doppler_bins - doppler_first) % AZ) < ABAND).astype(jnp.float32)
        band = doppler_keep[:, None] * range_keep[None, :]
        sec_filtered = jnp.fft.ifft2(jnp.fft.fft2(lax.complex(secondary[0], secondary[1])) * band)
        ref_filtered = jnp.fft.ifft2(ref_spectrum * band)
        product = sec_filtered * jnp.conj(ref_filtered)
        return jnp.stack([jnp.real(product), jnp.imag(product)], 0).astype(jnp.float32)

    return lax.map(one_date, (secondary_slc, range_start, azimuth_start))
```

```python
import math

import jax
import jax.numpy as jnp
import ml_dtypes
import numpy as np
from jax import lax
from jax.experimental import pallas as pl
from jax.experimental.pallas import tpu as pltpu
from jax.sharding import PartitionSpec as P

RG = 12288
AZ = 384
OUTER = 32
INNER = 384
KEEP = 256
LINES = 12
ROWS = 24
PEERS = 32
MESH = pl.DeviceIdType.MESH
F32 = jnp.float32
BF16 = jnp.bfloat16
VMEM_LIMIT = 56 * 1024 * 1024


def row_line():
    return np.array(list(range(8)) + list(range(8)) + list(range(8, 12)) * 2)


def row_part():
    return np.array([0] * 8 + [1] * 8 + [0] * 4 + [1] * 4)


def dirichlet(offset, width, length):
    offset = np.asarray(offset)
    safe = np.where(offset == 0, 1, offset)
    value = np.sin(np.pi * width * safe / length) / (length * np.sin(np.pi * safe / length))
    return np.where(offset == 0, width / length, value)


def split_table(table):
    table = np.asarray(table, np.float32)
    high = table.astype(ml_dtypes.bfloat16)
    low = (table - high.astype(np.float32)).astype(ml_dtypes.bfloat16)
    return np.stack([high, low])


def azimuth_tables():
    lines = (np.arange(PEERS)[:, None] * LINES + row_line()[None]).reshape(-1)
    part = np.tile(row_part(), PEERS)
    full = dirichlet(lines[:, None] - lines[None, :], AZ // 2, AZ)
    own = full * (part[:, None] == part[None, :])
    return split_table(own), full.astype(np.float32).reshape(4, 192, 768)


def range_tables():
    n2 = np.arange(INNER)
    angle = 2 * np.pi * (np.arange(KEEP // 2)[None, :] + 0.5) * n2[:, None] / INNER
    basis = math.sqrt(2 / INNER) * np.concatenate([np.cos(angle), np.sin(angle)], 1)
    projection = dirichlet(n2[:, None] - n2[None, :], KEEP, INNER)
    return split_table(basis), split_table(basis.T), split_table(projection)


def cmul_const(re, im, angle):
    c, s = math.cos(angle), math.sin(angle)
    if abs(c - 1) < 1e-12:
        return re, im
    if abs(c) < 1e-12:
        return (-im, re) if s > 0 else (im, -re)
    if abs(abs(c) - abs(s)) < 1e-12:
        r = math.sqrt(0.5)
        if c > 0 and s > 0:
            return (re - im) * r, (re + im) * r
        if c > 0:
            return (re + im) * r, (im - re) * r
        if s > 0:
            return (re + im) * -r, (re - im) * r
        return (im - re) * r, (re + im) * -r
    return re * c - im * s, re * s + im * c


def dft_small(values, sign):
    n = len(values)
    if n == 1:
        return values
    even = dft_small(values[0::2], sign)
    odd = dft_small(values[1::2], sign)
    low, high = [], []
    for k in range(n // 2):
        tr, ti = cmul_const(odd[k][0], odd[k][1], sign * 2 * math.pi * k / n)
        low.append((even[k][0] + tr, even[k][1] + ti))
        high.append((even[k][0] - tr, even[k][1] - ti))
    return low + high


def dft32(load, sign):
    middle = []
    for q in range(8):
        part = dft_small([load(q + 8 * p) for p in range(4)], sign)
        middle.append([cmul_const(*part[s], sign * 2 * math.pi * q * s / 32) for s in range(4)])
    out = [None] * 32
    for s in range(4):
        part = dft_small([middle[q][s] for q in range(8)], sign)
        for t in range(8):
            out[s + 4 * t] = part[t]
    return out


def split_value(x):
    high = x.astype(BF16)
    low = (x - high.astype(F32)).astype(BF16)
    return high, low


def dot(a, b):
    return jnp.dot(a, b, preferred_element_type=F32)


def dot3(a, b):
    return dot(a[0], b[0]) + dot(a[1], b[0]) + dot(a[0], b[1])


def forward_kernel(sec_ref, twist_ref, phase_ref, basis_ref, out_ref, mid_ref):
    def chunk(a, _):
        for group in range(2):
            lines = slice(0, 8) if group == 0 else slice(8, 12)
            pc = phase_ref[0, lines, :]
            ps = phase_ref[1, lines, :]

            def load(n1):
                at = pl.ds(pl.multiple_of((n1 * 3 + a) * 128, 128), 128)
                return sec_ref[0, 0, lines, at], sec_ref[0, 1, lines, at]

            for k1, (re, im) in enumerate(dft32(load, -1)):
                c = twist_ref[0, a, k1 : k1 + 1, :]
                s = twist_ref[1, a, k1 : k1 + 1, :]
                re, im = re * c + im * s, im * c - re * s
                re, im = re * pc + im * ps, im * pc - re * ps
                if group == 0:
                    mid_ref[a, k1 * ROWS : k1 * ROWS + 8, :] = re
                    mid_ref[a, k1 * ROWS + 8 : k1 * ROWS + 16, :] = im
                else:
                    mid_ref[a, k1 * ROWS + 16 : k1 * ROWS + 24, :] = jnp.concatenate([re, im], 0)
        return 0

    lax.fori_loop(0, 3, chunk, 0)

    def rows(step, _):
        at = pl.ds(pl.multiple_of(step * 192, 192), 192)
        block = jnp.concatenate([mid_ref[a, at, :] for a in range(3)], 1)
        result = dot3(split_value(block), (basis_ref[0], basis_ref[1]))
        out_ref[pl.ds(step * 8, 8)] = result.reshape(8, ROWS, KEEP)
        return 0

    lax.fori_loop(0, 4, rows, 0)


def forward(sec, twist, phase, basis):
    return pl.pallas_call(
        forward_kernel,
        out_shape=jax.ShapeDtypeStruct((PEERS, ROWS, KEEP), F32),
        scratch_shapes=[pltpu.VMEM((3, PEERS * ROWS, 128), F32)],
        compiler_params=pltpu.CompilerParams(vmem_limit_bytes=VMEM_LIMIT),
        name="range_forward",
    )(sec, twist, phase, basis)


def remote(src, dst, send, recv, date, line):
    return pltpu.make_async_remote_copy(
        src_ref=src, dst_ref=dst, send_sem=send, recv_sem=recv, device_id=(date, line), device_id_type=MESH
    )


def chunk_of(zh, y):
    skip = 3 - y
    return jnp.where(zh > skip, zh - 1, zh), zh != skip


def gather_kernel(
    sec_ref, chunks_ref, vec_ref, spread_ref, all_ref, vecs_ref,
    a_send, a_recv, v_send, v_recv, y_send, y_recv, r_send, r_recv, l_send, l_recv, own_sem,
):
    d, l = lax.axis_index("date"), lax.axis_index("line")
    x, zh = d // 4, d % 4
    zl, u = l // 8, l % 8
    y = u // 2
    z = zh * 4 + zl
    up, down = (z + 1) % 16, (z + 15) % 16
    right = (x * 4 + up // 4, (up % 4) * 8 + u)
    left = (x * 4 + down // 4, (down % 4) * 8 + u)

    barrier = pltpu.get_barrier_semaphore()

    def greet(i, _):
        pl.semaphore_signal(barrier, inc=1, device_id=(d, (l + i) % PEERS), device_id_type=MESH)
        return 0

    lax.fori_loop(1, PEERS, greet, 0)
    for i in range(1, 4):
        pl.semaphore_signal(barrier, inc=1, device_id=((x + i) % 4 * 4 + zh, l), device_id_type=MESH)
    pl.semaphore_signal(barrier, inc=1, device_id=right, device_id_type=MESH)
    pl.semaphore_signal(barrier, inc=1, device_id=left, device_id_type=MESH)
    pl.semaphore_wait(barrier, PEERS - 1 + 3 + 2)

    def y_copy(c, owner, source):
        return remote(
            chunks_ref.at[c],
            all_ref.at[(6 * zh + c) // 8, zl, pl.ds(pl.multiple_of(source * ROWS, 8), ROWS)],
            y_send.at[c], y_recv.at[source], d, zl * 8 + owner,
        )

    mine, valid = chunk_of(zh, y)
    for c in range(6):
        owner = (6 * zh + c) % 8

        @pl.when(owner != u)
        def _():
            y_copy(c, owner, u).start()

        @pl.when(owner == u)
        def _():
            pltpu.make_async_copy(
                chunks_ref.at[c],
                all_ref.at[(6 * zh + c) // 8, zl, pl.ds(pl.multiple_of(u * ROWS, 8), ROWS)],
                own_sem.at[0],
            ).start()

    def v_copy(i):
        return remote(vec_ref, vecs_ref.at[x], v_send.at[i], v_recv.at[x], (x + i) % 4 * 4 + zh, l)

    def v_arrival(i):
        return remote(
            vec_ref, vecs_ref.at[(x + i) % 4], v_send.at[i], v_recv.at[(x + i) % 4], (x + i) % 4 * 4 + zh, l
        )

    for i in range(1, 4):
        v_copy(i).start()
    own_vec = pltpu.make_async_copy(vec_ref, vecs_ref.at[x], own_sem.at[1])
    own_vec.start()
    own_block = pltpu.make_async_copy(sec_ref.at[l], spread_ref.at[l], own_sem.at[2])
    own_block.start()

    def a_copy(i):
        to = (l + i) % PEERS
        return remote(sec_ref.at[to], spread_ref.at[l], a_send.at[i], a_recv.at[l], d, to)

    def a_start(i, _):
        a_copy(i).start()
        return 0

    def y_arrival(i):
        source = (u + i) % 8
        return remote(
            chunks_ref.at[0],
            all_ref.at[mine, zl, pl.ds(pl.multiple_of(source * ROWS, 8), ROWS)],
            y_send.at[0], y_recv.at[source], d, zl * 8 + source,
        )

    lax.fori_loop(1, PEERS, a_start, 0)

    @pl.when(valid)
    def _():
        for i in range(1, 8):
            y_arrival(i).wait_recv()
        pltpu.make_async_copy(
            chunks_ref.at[0],
            all_ref.at[mine, zl, pl.ds(pl.multiple_of(u * ROWS, 8), ROWS)],
            own_sem.at[0],
        ).wait()

    def ring_copy(origin, send, recv, step, to):
        oh, ol = origin // 4, origin % 4
        i, ok = chunk_of(oh, y)
        i = jnp.where(ok, i, 0)
        return ok, remote(all_ref.at[i, ol], all_ref.at[i, ol], send.at[step], recv.at[step], *to)

    def ring(s, _):
        ok, copy = ring_copy((z + 17 - s) % 16, r_send, r_recv, s, right)

        @pl.when(ok)
        def _():
            copy.start()

        ok2, copy2 = ring_copy((z + s - 1) % 16, l_send, l_recv, s, left)

        @pl.when(ok2 & (s < 8))
        def _():
            copy2.start()

        ok3, copy3 = ring_copy((z + 16 - s) % 16, r_send, r_recv, s, left)

        @pl.when(ok3)
        def _():
            copy3.wait_recv()

        ok4, copy4 = ring_copy((z + s) % 16, l_send, l_recv, s, right)

        @pl.when(ok4 & (s < 8))
        def _():
            copy4.wait_recv()

        return 0

    lax.fori_loop(1, 9, ring, 0)

    def ring_sent(s, _):
        ok, copy = ring_copy((z + 17 - s) % 16, r_send, r_recv, s, right)

        @pl.when(ok)
        def _():
            copy.wait_send()

        ok2, copy2 = ring_copy((z + s - 1) % 16, l_send, l_recv, s, left)

        @pl.when(ok2 & (s < 8))
        def _():
            copy2.wait_send()

        return 0

    lax.fori_loop(1, 9, ring_sent, 0)

    for c in range(6):
        owner = (6 * zh + c) % 8

        @pl.when(owner != u)
        def _():
            y_copy(c, owner, u).wait_send()

    for i in range(1, 4):
        v_copy(i).wait_send()
        v_arrival(i).wait_recv()
    own_vec.wait()
    own_block.wait()

    def a_finish(i, _):
        a_copy(i).wait_send()
        source = (l + i) % PEERS
        remote(sec_ref.at[source], spread_ref.at[source], a_send.at[i], a_recv.at[source], d, source).wait_recv()
        return 0

    lax.fori_loop(1, PEERS, a_finish, 0)


def gather(sec_blocks, chunks, vector):
    any_space = pl.BlockSpec(memory_space=pl.ANY)
    dma = pltpu.SemaphoreType.DMA
    return pl.pallas_call(
        gather_kernel,
        out_shape=(
            jax.ShapeDtypeStruct((PEERS, ROWS, KEEP), F32),
            jax.ShapeDtypeStruct((3, 4, 8 * ROWS, 128), F32),
            jax.ShapeDtypeStruct((4, 8, 2 * AZ), F32),
        ),
        in_specs=[any_space] * 3,
        out_specs=(any_space,) * 3,
        scratch_shapes=[
            dma((PEERS,)), dma((PEERS,)), dma((4,)), dma((4,)), dma((6,)), dma((8,)),
            dma((9,)), dma((9,)), dma((9,)), dma((9,)), dma((3,)),
        ],
        compiler_params=pltpu.CompilerParams(collective_id=1, has_side_effects=True),
        name="gather_lines",
    )(sec_blocks, chunks, vector)


def return_kernel(
    sec_ref, ref_ref, spread_ref, lines_ref, a_send, a_recv, x_send, x_recv, own_sem
):
    d, l = lax.axis_index("date"), lax.axis_index("line")
    x, zh = d // 4, d % 4
    zl, u = l // 8, l % 8
    place = x * 8 + u

    def plane(i):
        other = (place + i) % PEERS
        ox, ou = other // 8, other % 8
        return other, ox, ou, ox * 4 + zh, zl * 8 + ou

    barrier = pltpu.get_barrier_semaphore()

    def greet(i, _):
        pl.semaphore_signal(barrier, inc=1, device_id=(d, (l + i) % PEERS), device_id_type=MESH)
        _, _, _, od, ol = plane(i)
        pl.semaphore_signal(barrier, inc=1, device_id=(od, ol), device_id_type=MESH)
        return 0

    lax.fori_loop(1, PEERS, greet, 0)
    pl.semaphore_wait(barrier, 2 * (PEERS - 1))

    own_block = pltpu.make_async_copy(sec_ref.at[l], spread_ref.at[l], own_sem.at[0])
    own_block.start()
    own_lines = pltpu.make_async_copy(ref_ref.at[x, u], lines_ref.at[x, :, u], own_sem.at[1])
    own_lines.start()

    def a_copy(i):
        to = (l + i) % PEERS
        return remote(sec_ref.at[to], spread_ref.at[l], a_send.at[i], a_recv.at[l], d, to)

    def x_copy(i):
        _, ox, ou, od, ol = plane(i)
        return remote(ref_ref.at[ox, ou], lines_ref.at[x, :, u], x_send.at[i], x_recv.at[place], od, ol)

    def start(i, _):
        a_copy(i).start()
        x_copy(i).start()
        return 0

    lax.fori_loop(1, PEERS, start, 0)
    own_block.wait()
    own_lines.wait()

    def finish(i, _):
        a_copy(i).wait_send()
        x_copy(i).wait_send()
        source = (l + i) % PEERS
        remote(sec_ref.at[source], spread_ref.at[source], a_send.at[i], a_recv.at[source], d, source).wait_recv()
        other, ox, ou, od, ol = plane(i)
        remote(ref_ref.at[ox, ou], lines_ref.at[ox, :, ou], x_send.at[i], x_recv.at[other], od, ol).wait_recv()
        return 0

    lax.fori_loop(1, PEERS, finish, 0)


def give_back(sec_blocks, ref_blocks):
    any_space = pl.BlockSpec(memory_space=pl.ANY)
    dma = pltpu.SemaphoreType.DMA
    return pl.pallas_call(
        return_kernel,
        out_shape=(
            jax.ShapeDtypeStruct((PEERS, ROWS, KEEP), F32),
            jax.ShapeDtypeStruct((4, 3, 8, ROWS, 128), F32),
        ),
        in_specs=[any_space] * 2,
        out_specs=(any_space,) * 2,
        scratch_shapes=[dma((PEERS,)), dma((PEERS,)), dma((PEERS,)), dma((PEERS,)), dma((2,))],
        compiler_params=pltpu.CompilerParams(collective_id=2, has_side_effects=True),
        name="return_lines",
    )(sec_blocks, ref_blocks)


def azimuth_kernel(sec_ref, all_ref, vecs_ref, own_ref, full_ref, sec_out, ref_out):
    def sec_rows(step, _):
        at = pl.ds(pl.multiple_of(step * 192, 192), 192)
        result = dot3((own_ref[0, at, :], own_ref[1, at, :]), sec)
        sec_out[pl.ds(step * 8, 8)] = result.reshape(8, ROWS, KEEP)
        return 0

    sec = split_value(sec_ref[...].reshape(PEERS * ROWS, KEEP))
    lax.fori_loop(0, 4, sec_rows, 0)
    samples = split_value(
        jnp.concatenate([all_ref[i].reshape(2 * AZ, 128) for i in range(3)], 1)
    )
    row = lax.broadcasted_iota(jnp.int32, (ROWS, 2 * AZ), 0)
    real = (row < 8) | ((row >= 16) & (row < 20))

    def date(t, _):
        first = vecs_ref[t, 0:1, :]
        second = vecs_ref[t, 1:2, :]
        mixed = jnp.where(real, first, second)
        table = full_ref[...].reshape(8, ROWS, 2 * AZ) * mixed[None]
        result = dot3(split_value(table.reshape(8 * ROWS, 2 * AZ)), samples)
        for i in range(3):
            ref_out[t, :, i] = result[:, i * 128 : (i + 1) * 128].reshape(8, ROWS, 128)
        return 0

    lax.fori_loop(0, 4, date, 0)


def azimuth(spread, every, vectors, own, full):
    return pl.pallas_call(
        azimuth_kernel,
        out_shape=(
            jax.ShapeDtypeStruct((PEERS, ROWS, KEEP), F32),
            jax.ShapeDtypeStruct((4, 8, 3, ROWS, 128), F32),
        ),
        compiler_params=pltpu.CompilerParams(vmem_limit_bytes=VMEM_LIMIT),
        name="azimuth_filter",
    )(spread, every, vectors, own, full)


def final_kernel(sec_ref, lines_ref, twist_ref, inverse_ref, project_ref, out_ref, sec_mid, ref_mid, sec_time):
    def sec_rows(step, _):
        at = pl.ds(pl.multiple_of(step * 192, 192), 192)
        block = split_value(sec_ref[pl.ds(step * 8, 8)].reshape(192, KEEP))
        result = dot3(block, (inverse_ref[0], inverse_ref[1]))
        for a in range(3):
            sec_mid[a, at, :] = result[:, a * 128 : (a + 1) * 128]
        return 0

    lax.fori_loop(0, 4, sec_rows, 0)

    def pair(tile, group):
        return pltpu.roll(tile, 4, 0) if group else None

    def forward_chunk(a, _):
        for group in range(2):

            def load(n1):
                if group == 0:
                    return lines_ref[n1 * 3 + a, 0:8, :], lines_ref[n1 * 3 + a, 8:16, :]
                tile = lines_ref[n1 * 3 + a, 16:24, :]
                return tile, pair(tile, 1)

            for k1, (re, im) in enumerate(dft32(load, -1)):
                c = twist_ref[0, a, k1 : k1 + 1, :]
                s = twist_ref[1, a, k1 : k1 + 1, :]
                re, im = re * c + im * s, im * c - re * s
                base = k1 * ROWS
                if group == 0:
                    ref_mid[a, base : base + 8, :] = re
                    ref_mid[a, base + 8 : base + 16, :] = im
                else:
                    ref_mid[a, base + 16 : base + 24, :] = jnp.concatenate([re[0:4], im[0:4]], 0)
        return 0

    lax.fori_loop(0, 3, forward_chunk, 0)

    def ref_rows(step, _):
        at = pl.ds(pl.multiple_of(step * 192, 192), 192)
        block = jnp.concatenate([ref_mid[a, at, :] for a in range(3)], 1)
        result = dot3(split_value(block), (project_ref[0], project_ref[1]))
        for a in range(3):
            ref_mid[a, at, :] = result[:, a * 128 : (a + 1) * 128]
        return 0

    lax.fori_loop(0, 4, ref_rows, 0)

    def untwist(mid, a, group):
        def load(k1):
            base = k1 * ROWS
            c = twist_ref[0, a, k1 : k1 + 1, :]
            s = twist_ref[1, a, k1 : k1 + 1, :]
            if group == 0:
                re, im = mid[a, base : base + 8, :], mid[a, base + 8 : base + 16, :]
            else:
                re = mid[a, base + 16 : base + 24, :]
                im = pair(re, 1)
            return re * c - im * s, im * c + re * s

        return load

    def last_chunk(a, _):
        for group in range(2):
            count = 8 if group == 0 else 4
            lines = slice(0, 8) if group == 0 else slice(8, 12)
            for n1, (re, im) in enumerate(dft32(untwist(sec_mid, a, group), 1)):
                sec_time[0, n1] = re
                sec_time[1, n1] = im
            for n1, (re, im) in enumerate(dft32(untwist(ref_mid, a, group), 1)):
                sr = sec_time[0, n1] * (1.0 / 1024)
                si = sec_time[1, n1] * (1.0 / 1024)
                at = pl.ds(pl.multiple_of((n1 * 3 + a) * 128, 128), 128)
                out_ref[0, 0, lines, at] = (sr * re + si * im)[0:count]
                out_ref[0, 1, lines, at] = (si * re - sr * im)[0:count]
        return 0

    lax.fori_loop(0, 3, last_chunk, 0)


def final(sec_blocks, lines, twist, inverse, project):
    return pl.pallas_call(
        final_kernel,
        out_shape=jax.ShapeDtypeStruct((1, 2, LINES, RG), F32),
        scratch_shapes=[
            pltpu.VMEM((3, PEERS * ROWS, 128), F32),
            pltpu.VMEM((3, PEERS * ROWS, 128), F32),
            pltpu.VMEM((2, OUTER, 8, 128), F32),
        ],
        compiler_params=pltpu.CompilerParams(vmem_limit_bytes=VMEM_LIMIT),
        name="range_final",
    )(sec_blocks, lines, twist, inverse, project)


def body(reference_slc, secondary_slc, range_start, azimuth_start):
    own, full = azimuth_tables()
    basis, inverse, project = range_tables()
    line = lax.axis_index("line")

    first = range_start[0] + (jnp.arange(OUTER, dtype=jnp.int32) - range_start[0]) % OUTER
    turns = (first + OUTER * (KEEP - 1) // 2)[None, :, None] * jnp.arange(INNER, dtype=jnp.int32).reshape(3, 1, 128)
    angle = (turns % RG).astype(F32) * (2 * math.pi / RG)
    twist = jnp.stack([jnp.cos(angle), jnp.sin(angle)])

    step = 2 * azimuth_start[0] + AZ // 2 - 1

    def phases(lines):
        angle = ((step * lines) % (2 * AZ)).astype(F32) * (math.pi / AZ)
        return jnp.cos(angle), jnp.sin(angle)

    own_cos, own_sin = phases(line * LINES + jnp.arange(LINES, dtype=jnp.int32))
    phase = jnp.broadcast_to(jnp.stack([own_cos, own_sin])[:, :, None], (2, LINES, 128))
    all_rows = (np.arange(PEERS)[:, None] * LINES + row_line()[None]).reshape(-1).astype(np.int32)
    all_real = np.tile(row_part() == 0, PEERS)
    row_cos, row_sin = phases(jnp.asarray(all_rows))
    vector = jnp.stack([jnp.where(all_real, row_cos, row_sin), jnp.where(all_real, -row_sin, row_cos)])
    vector = jnp.pad(vector, ((0, 6), (0, 0)))

    parts = reference_slc.reshape(2, LINES, 6, 128).transpose(2, 0, 1, 3)
    chunks = jnp.concatenate([parts[:, 0, :8], parts[:, 1, :8], parts[:, 0, 8:], parts[:, 1, 8:]], 1)

    full_here = lax.dynamic_index_in_dim(jnp.asarray(full), line // 8, 0, keepdims=False)
    coefficients = forward(secondary_slc, twist, phase, jnp.asarray(basis))
    spread, every, vectors = gather(coefficients, chunks, vector)
    filtered, ref_filtered = azimuth(spread, every, vectors, jnp.asarray(own), full_here)
    returned, lines = give_back(filtered, ref_filtered)
    lines = lines.reshape(96, ROWS, 128)
    return final(returned, lines, twist, jnp.asarray(inverse), jnp.asarray(project))


def solution(mesh):
    in_specs = (P(None, "line", "date"), P("date", None, "line", None), P("date"), P("date"))
    out_specs = P("date", None, "line", None)
    return jax.shard_map(body, mesh=mesh, in_specs=in_specs, out_specs=out_specs, check_vma=False)
```

```python
import math

import jax
import jax.numpy as jnp
import ml_dtypes
import numpy as np
from jax import lax
from jax.experimental import pallas as pl
from jax.experimental.pallas import tpu as pltpu
from jax.sharding import PartitionSpec as P

RG = 12288
AZ = 384
OUTER = 32
INNER = 384
KEEP = 256
LINES = 12
ROWS = 24
PEERS = 32
MESH = pl.DeviceIdType.MESH
F32 = jnp.float32
BF16 = jnp.bfloat16
VMEM_LIMIT = 56 * 1024 * 1024


def row_line():
    return np.array(list(range(8)) + list(range(8)) + list(range(8, 12)) * 2)


def row_part():
    return np.array([0] * 8 + [1] * 8 + [0] * 4 + [1] * 4)


def dirichlet(offset, width, length):
    offset = np.asarray(offset)
    safe = np.where(offset == 0, 1, offset)
    value = np.sin(np.pi * width * safe / length) / (length * np.sin(np.pi * safe / length))
    return np.where(offset == 0, width / length, value)


def split_table(table):
    table = np.asarray(table, np.float32)
    high = table.astype(ml_dtypes.bfloat16)
    low = (table - high.astype(np.float32)).astype(ml_dtypes.bfloat16)
    return np.stack([high, low])


def azimuth_tables():
    lines = (np.arange(PEERS)[:, None] * LINES + row_line()[None]).reshape(-1)
    part = np.tile(row_part(), PEERS)
    full = dirichlet(lines[:, None] - lines[None, :], AZ // 2, AZ)
    own = full * (part[:, None] == part[None, :])
    return split_table(own), full.astype(np.float32).reshape(4, 192, 768)


def range_tables():
    n2 = np.arange(INNER)
    angle = 2 * np.pi * (np.arange(KEEP // 2)[None, :] + 0.5) * n2[:, None] / INNER
    basis = math.sqrt(2 / INNER) * np.concatenate([np.cos(angle), np.sin(angle)], 1)
    projection = dirichlet(n2[:, None] - n2[None, :], KEEP, INNER)
    return split_table(basis), split_table(basis.T), split_table(projection)


def cmul_const(re, im, angle):
    c, s = math.cos(angle), math.sin(angle)
    if abs(c - 1) < 1e-12:
        return re, im
    if abs(c) < 1e-12:
        return (-im, re) if s > 0 else (im, -re)
    if abs(abs(c) - abs(s)) < 1e-12:
        r = math.sqrt(0.5)
        if c > 0 and s > 0:
            return (re - im) * r, (re + im) * r
        if c > 0:
            return (re + im) * r, (im - re) * r
        if s > 0:
            return (re + im) * -r, (re - im) * r
        return (im - re) * r, (re + im) * -r
    return re * c - im * s, re * s + im * c


def dft_small(values, sign):
    n = len(values)
    if n == 1:
        return values
    even = dft_small(values[0::2], sign)
    odd = dft_small(values[1::2], sign)
    low, high = [], []
    for k in range(n // 2):
        tr, ti = cmul_const(odd[k][0], odd[k][1], sign * 2 * math.pi * k / n)
        low.append((even[k][0] + tr, even[k][1] + ti))
        high.append((even[k][0] - tr, even[k][1] - ti))
    return low + high


def dft32(load, sign):
    middle = []
    for q in range(8):
        part = dft_small([load(q + 8 * p) for p in range(4)], sign)
        middle.append([cmul_const(*part[s], sign * 2 * math.pi * q * s / 32) for s in range(4)])
    out = [None] * 32
    for s in range(4):
        part = dft_small([middle[q][s] for q in range(8)], sign)
        for t in range(8):
            out[s + 4 * t] = part[t]
    return out


def split_value(x):
    high = x.astype(BF16)
    low = (x - high.astype(F32)).astype(BF16)
    return high, low


def dot(a, b):
    return jnp.dot(a, b, preferred_element_type=F32)


def dot3(a, b):
    return dot(a[0], b[0]) + dot(a[1], b[0]) + dot(a[0], b[1])


TWIST, VECTOR, PHASE, TRIG = 0, 192, 208, 240


def trig_tables():
    index = np.zeros((TRIG, 128), np.int32)
    residue = np.full((TRIG, 128), -1, np.int32)
    offset = np.zeros((TRIG, 128), np.int32)
    for part in range(2):
        for a in range(3):
            for k1 in range(OUTER):
                row = part * 96 + a * OUTER + k1
                index[row] = a * 128 + np.arange(128)
                residue[row] = k1
                offset[row] = -part * RG // 4
    lines = (np.arange(PEERS)[:, None] * LINES + row_line()[None]).reshape(6, 128)
    real = np.tile(row_part() == 0, PEERS).reshape(6, 128)
    index[VECTOR : VECTOR + 6] = lines
    offset[VECTOR : VECTOR + 6] = np.where(real, 0, -RG // 4)
    index[VECTOR + 8 : VECTOR + 14] = lines
    offset[VECTOR + 8 : VECTOR + 14] = np.where(real, RG // 4, 0)
    for part in range(2):
        for i in range(LINES):
            row = PHASE + part * 16 + i
            index[row] = i
            residue[row] = -2
            offset[row] = -part * RG // 4
    return index, residue, offset


def trig_values(range_first, azimuth_first, line):
    index, residue, offset = (jnp.asarray(t) for t in trig_tables())
    index = jnp.where(residue == -2, index + line * LINES, index)
    bins = range_first + (residue - range_first) % OUTER + OUTER * (KEEP - 1) // 2
    factor = jnp.where(residue >= 0, bins, (RG // (2 * AZ)) * (2 * azimuth_first + AZ // 2 - 1))
    turns = (factor * index + offset) % RG
    return jnp.cos(turns.astype(F32) * (2 * math.pi / RG))


def remote(src, dst, send, recv, date, line):
    return pltpu.make_async_remote_copy(
        src_ref=src, dst_ref=dst, send_sem=send, recv_sem=recv, device_id=(date, line), device_id_type=MESH
    )


def chunk_of(zh, y):
    skip = 3 - y
    return jnp.where(zh > skip, zh - 1, zh), zh != skip


def twiddle(trig_ref, a, k1):
    row = a * OUTER + k1
    return trig_ref[pl.ds(row, 1), :], trig_ref[pl.ds(96 + row, 1), :]


PIECES = 2
PIECE = 8 * ROWS // PIECES
STEPS = 8


def exchange_kernel(
    sec_ref, refr_ref, trig_ref, basis_ref, own_hbm, full_hbm, back_ref, lines_ref,
    mid_ref, coef_ref, spread_ref, chunks_ref, all_ref, vecs_ref, filt_ref, rout_ref, own_ref, full_ref,
    a_send, a_recv, b_send, b_recv, x_send, x_recv, v_send, v_recv, y_send, y_recv,
    r_send, r_recv, l_send, l_recv, own_sem,
):
    d, l = lax.axis_index("date"), lax.axis_index("line")
    x, zh = d // 4, d % 4
    zl, u = l // 8, l % 8
    y = u // 2
    z = zh * 4 + zl
    up, down = (z + 1) % 16, (z + 15) % 16
    right = (x * 4 + up // 4, (up % 4) * 8 + u)
    left = (x * 4 + down // 4, (down % 4) * 8 + u)
    place = x * 8 + u
    mine, valid = chunk_of(zh, y)

    own_copy = pltpu.make_async_copy(own_hbm, own_ref, own_sem.at[4])
    own_copy.start()
    full_copy = pltpu.make_async_copy(full_hbm.at[zl], full_ref, own_sem.at[5])
    full_copy.start()

    def plane(i):
        other = (place + i) % PEERS
        ox, ou = other // 8, other % 8
        return other, ox, ou, ox * 4 + zh, zl * 8 + ou

    barrier = pltpu.get_barrier_semaphore()

    def greet(i, _):
        pl.semaphore_signal(barrier, inc=1, device_id=(d, (l + i) % PEERS), device_id_type=MESH)
        _, _, _, od, ol = plane(i)
        pl.semaphore_signal(barrier, inc=1, device_id=(od, ol), device_id_type=MESH)
        return 0

    pl.semaphore_signal(barrier, inc=1, device_id=right, device_id_type=MESH)
    pl.semaphore_signal(barrier, inc=1, device_id=left, device_id_type=MESH)
    lax.fori_loop(1, PEERS, greet, 0)

    for c in range(6):
        for part in range(2):
            chunks_ref[c, part * 8 : part * 8 + 8, :] = refr_ref[pl.ds(c * 2 + part, 8, stride=12), :]
            chunks_ref[c, 16 + part * 4 : 20 + part * 4, :] = refr_ref[pl.ds(96 + c * 2 + part, 4, stride=12), :]

    pl.semaphore_wait(barrier, 2 * (PEERS - 1) + 2)

    def y_slot(i, source):
        return all_ref.at[i, zl, pl.ds(pl.multiple_of(source * ROWS, 8), ROWS)]

    def y_copy(c):
        q = 6 * zh + c
        return remote(chunks_ref.at[c], y_slot(q // 8, u), y_send.at[c], y_recv.at[u], d, zl * 8 + q % 8)

    def y_own(c):
        return pltpu.make_async_copy(chunks_ref.at[c], y_slot((6 * zh + c) // 8, u), own_sem.at[0])

    for c in range(6):
        owner = (6 * zh + c) % 8

        @pl.when(owner != u)
        def _():
            y_copy(c).start()

        @pl.when(owner == u)
        def _():
            y_own(c).start()

    def v_copy(i, slot):
        return remote(
            trig_ref.at[pl.ds(VECTOR, 16)], vecs_ref.at[slot], v_send.at[i], v_recv.at[slot],
            (x + i) % 4 * 4 + zh, l,
        )

    for i in range(1, 4):
        v_copy(i, x).start()
    own_vec = pltpu.make_async_copy(trig_ref.at[pl.ds(VECTOR, 16)], vecs_ref.at[x], own_sem.at[1])
    own_vec.start()

    def chunk(a, _):
        for group in range(2):
            rows = 8 if group == 0 else 4
            first = 8 * group
            pc = trig_ref[PHASE + first : PHASE + first + rows, :]
            ps = trig_ref[PHASE + 16 + first : PHASE + 16 + first + rows, :]

            def load(n1):
                at = first * 192 + (n1 * 3 + a) * 2
                return sec_ref[pl.ds(at, rows, stride=192), :], sec_ref[pl.ds(at + 1, rows, stride=192), :]

            for k1, (re, im) in enumerate(dft32(load, -1)):
                c, s = twiddle(trig_ref, a, k1)
                re, im = re * c + im * s, im * c - re * s
                re, im = re * pc + im * ps, im * pc - re * ps
                if group == 0:
                    mid_ref[a, k1 * ROWS : k1 * ROWS + 8, :] = re
                    mid_ref[a, k1 * ROWS + 8 : k1 * ROWS + 16, :] = im
                else:
                    mid_ref[a, k1 * ROWS + 16 : k1 * ROWS + 24, :] = jnp.concatenate([re, im], 0)
        return 0

    def ring_copy(origin, send, recv, step, piece, to):
        i, ok = chunk_of(origin // 4, y)
        ref = all_ref.at[jnp.where(ok, i, 0), origin % 4, pl.ds(pl.multiple_of(piece * PIECE, 8), PIECE)]
        at = step * PIECES + piece
        return ok, remote(ref, ref, send.at[at], recv.at[at], *to)

    def ring_start(s, p):
        ok, copy = ring_copy((z + 17 - s) % 16, r_send, r_recv, s, p, right)
        pl.when(ok)(copy.start)
        ok2, copy2 = ring_copy((z + s - 1) % 16, l_send, l_recv, s, p, left)
        pl.when(ok2 & (s < STEPS))(copy2.start)

    def ring_sent(j, _):
        s, p = 1 + j // PIECES, j % PIECES
        ok, copy = ring_copy((z + 17 - s) % 16, r_send, r_recv, s, p, right)
        pl.when(ok)(copy.wait_send)
        ok2, copy2 = ring_copy((z + s - 1) % 16, l_send, l_recv, s, p, left)
        pl.when(ok2 & (s < STEPS))(copy2.wait_send)
        return 0

    def ring_arrived(s, p):
        ok, copy = ring_copy((z + 16 - s) % 16, r_send, r_recv, s, p, left)
        pl.when(ok)(copy.wait_recv)
        ok2, copy2 = ring_copy((z + s) % 16, l_send, l_recv, s, p, right)
        pl.when(ok2 & (s < STEPS))(copy2.wait_recv)

    def a_copy(i):
        to = (l + i) % PEERS
        return remote(coef_ref.at[to], spread_ref.at[l], a_send.at[i], a_recv.at[l], d, to)

    chunk(0, 0)

    @pl.when(valid)
    def _():
        for i in range(1, 8):
            source = (u + i) % 8
            remote(
                chunks_ref.at[0], y_slot(mine, source), y_send.at[0], y_recv.at[source], d, zl * 8 + source
            ).wait_recv()
        y_own(0).wait()

    for p in range(PIECES):
        ring_start(1, p)

    lax.fori_loop(1, 3, chunk, 0)

    for p in range(PIECES):
        ring_arrived(1, p)
        ring_start(2, p)

    def rows(step, _):
        at = pl.ds(pl.multiple_of(step * 192, 192), 192)
        block = jnp.concatenate([mid_ref[a, at, :] for a in range(3)], 1)
        result = dot3(split_value(block), (basis_ref[0], basis_ref[1]))
        coef_ref[pl.ds(step * 8, 8)] = result.reshape(8, ROWS, KEEP)
        return 0

    lax.fori_loop(0, 4, rows, 0)
    own_block = pltpu.make_async_copy(coef_ref.at[l], spread_ref.at[l], own_sem.at[2])
    own_block.start()

    def a_start(i, _):
        a_copy(i).start()
        return 0

    def ring(j, _):
        s, p = 2 + j // PIECES, j % PIECES
        ring_arrived(s, p)
        ring_start(s + 1, p)
        lax.fori_loop(1 + j * 31 // (6 * PIECES), 1 + (j + 1) * 31 // (6 * PIECES), a_start, 0)
        return 0

    lax.fori_loop(0, 6 * PIECES, ring, 0)
    for p in range(PIECES):
        ring_arrived(STEPS, p)
    lax.fori_loop(0, STEPS * PIECES, ring_sent, 0)
    for i in range(1, 4):
        v_copy(i, x).wait_send()
        v_copy(i, (x + i) % 4).wait_recv()
    own_vec.wait()
    full_copy.wait()

    samples = split_value(jnp.concatenate([all_ref[i].reshape(2 * AZ, 128) for i in range(3)], 1))
    row = lax.broadcasted_iota(jnp.int32, (ROWS, 128), 0)
    real = (row < 8) | ((row >= 16) & (row < 20))

    def x_copy(t, ou):
        return remote(
            rout_ref.at[t, ou], lines_ref.at[x, :, u], x_send.at[t * 8 + ou], x_recv.at[place],
            t * 4 + zh, zl * 8 + ou,
        )

    def x_own():
        return pltpu.make_async_copy(rout_ref.at[x, u], lines_ref.at[x, :, u], own_sem.at[3])

    def date(k, _):
        t = (x + 1 + k) % 4
        parts = []
        for j in range(6):
            mixed = jnp.where(real, vecs_ref[t, j : j + 1, :], vecs_ref[t, 8 + j : 9 + j, :])
            part = full_ref[:, j * 128 : (j + 1) * 128].reshape(8, ROWS, 128) * mixed[None]
            parts.append(part.reshape(8 * ROWS, 128))
        result = dot3(split_value(jnp.concatenate(parts, 1)), samples)
        for i in range(3):
            rout_ref[t, :, i] = result[:, i * 128 : (i + 1) * 128].reshape(8, ROWS, 128)

        def send(i, _):
            ou = (u + i) % 8
            away = (t != x) | (ou != u)
            pl.when(away)(x_copy(t, ou).start)
            return 0

        lax.fori_loop(0, 8, send, 0)
        return 0

    lax.fori_loop(0, 4, date, 0)
    x_own().start()

    def a_finish(i, _):
        a_copy(i).wait_send()
        source = (l + i) % PEERS
        remote(coef_ref.at[source], spread_ref.at[source], a_send.at[i], a_recv.at[source], d, source).wait_recv()
        return 0

    own_block.wait()
    own_copy.wait()
    lax.fori_loop(1, PEERS, a_finish, 0)
    sec = split_value(spread_ref[...].reshape(PEERS * ROWS, KEEP))

    def b_copy(to):
        return remote(filt_ref.at[to], back_ref.at[l], b_send.at[to], b_recv.at[l], d, to)

    def b_own():
        return pltpu.make_async_copy(filt_ref.at[l], back_ref.at[l], own_sem.at[2])

    def sec_rows(k, _):
        step = (zl + 1 + k) % 4
        at = pl.ds(pl.multiple_of(step * 192, 192), 192)
        result = dot3((own_ref[0, at, :], own_ref[1, at, :]), sec)
        filt_ref[pl.ds(step * 8, 8)] = result.reshape(8, ROWS, KEEP)

        def send(i, _):
            to = step * 8 + (u + i) % 8
            pl.when(to != l)(b_copy(to).start)
            return 0

        lax.fori_loop(0, 8, send, 0)
        return 0

    lax.fori_loop(0, 4, sec_rows, 0)
    b_own().start()

    for c in range(6):
        owner = (6 * zh + c) % 8

        @pl.when(owner != u)
        def _():
            y_copy(c).wait_send()

    def finish(i, _):
        other, ox, ou, od, ol = plane(i)
        x_copy(ox, ou).wait_send()
        remote(rout_ref.at[ox, ou], lines_ref.at[ox, :, ou], x_send.at[other], x_recv.at[other], od, ol).wait_recv()
        source = (l + i) % PEERS
        b_copy(source).wait_send()
        remote(filt_ref.at[source], back_ref.at[source], b_send.at[source], b_recv.at[source], d, source).wait_recv()
        return 0

    x_own().wait()
    b_own().wait()
    lax.fori_loop(1, PEERS, finish, 0)


def exchange(sec, ref, trig, basis, own, full):
    any_space = pl.BlockSpec(memory_space=pl.ANY)
    vmem = pl.BlockSpec(memory_space=pltpu.VMEM)
    dma = pltpu.SemaphoreType.DMA
    blocks = (PEERS, ROWS, KEEP)
    ring = (STEPS + 1) * PIECES
    return pl.pallas_call(
        exchange_kernel,
        out_shape=(jax.ShapeDtypeStruct(blocks, F32), jax.ShapeDtypeStruct((4, 3, 8, ROWS, 128), F32)),
        in_specs=[vmem] * 4 + [any_space] * 2,
        out_specs=(any_space,) * 2,
        scratch_shapes=[
            pltpu.VMEM((3, PEERS * ROWS, 128), F32),
            pltpu.VMEM(blocks, F32),
            pltpu.VMEM(blocks, F32),
            pltpu.VMEM((6, ROWS, 128), F32),
            pltpu.VMEM((3, 4, 8 * ROWS, 128), F32),
            pltpu.VMEM((4, 16, 128), F32),
            pltpu.VMEM(blocks, F32),
            pltpu.VMEM((4, 8, 3, ROWS, 128), F32),
            pltpu.VMEM((2, 2 * AZ, 2 * AZ), BF16),
            pltpu.VMEM((8 * ROWS, 2 * AZ), F32),
            dma((PEERS,)), dma((PEERS,)), dma((PEERS,)), dma((PEERS,)), dma((PEERS,)), dma((PEERS,)),
            dma((4,)), dma((4,)), dma((6,)), dma((8,)),
            dma((ring,)), dma((ring,)), dma((ring,)), dma((ring,)), dma((6,)),
        ],
        compiler_params=pltpu.CompilerParams(
            collective_id=1, has_side_effects=True, vmem_limit_bytes=VMEM_LIMIT
        ),
        name="exchange",
    )(sec, ref, trig, basis, own, full)


def final_kernel(sec_ref, lines_ref, trig_ref, inverse_ref, project_ref, out_ref, sec_mid, ref_mid, sec_time):
    def sec_rows(step, _):
        at = pl.ds(pl.multiple_of(step * 192, 192), 192)
        block = split_value(sec_ref[pl.ds(step * 8, 8)].reshape(192, KEEP))
        result = dot3(block, (inverse_ref[0], inverse_ref[1]))
        for a in range(3):
            sec_mid[a, at, :] = result[:, a * 128 : (a + 1) * 128]
        return 0

    lax.fori_loop(0, 4, sec_rows, 0)

    def pair(tile, group):
        return pltpu.roll(tile, 4, 0) if group else None

    def forward_chunk(a, _):
        for group in range(2):

            def load(n1):
                if group == 0:
                    return lines_ref[n1 * 3 + a, 0:8, :], lines_ref[n1 * 3 + a, 8:16, :]
                tile = lines_ref[n1 * 3 + a, 16:24, :]
                return tile, pair(tile, 1)

            for k1, (re, im) in enumerate(dft32(load, -1)):
                c, s = twiddle(trig_ref, a, k1)
                re, im = re * c + im * s, im * c - re * s
                base = k1 * ROWS
                if group == 0:
                    ref_mid[a, base : base + 8, :] = re
                    ref_mid[a, base + 8 : base + 16, :] = im
                else:
                    ref_mid[a, base + 16 : base + 24, :] = jnp.concatenate([re[0:4], im[0:4]], 0)
        return 0

    lax.fori_loop(0, 3, forward_chunk, 0)

    def ref_rows(step, _):
        at = pl.ds(pl.multiple_of(step * 192, 192), 192)
        block = jnp.concatenate([ref_mid[a, at, :] for a in range(3)], 1)
        result = dot3(split_value(block), (project_ref[0], project_ref[1]))
        for a in range(3):
            ref_mid[a, at, :] = result[:, a * 128 : (a + 1) * 128]
        return 0

    lax.fori_loop(0, 4, ref_rows, 0)

    def untwist(mid, a, group):
        def load(k1):
            base = k1 * ROWS
            c, s = twiddle(trig_ref, a, k1)
            if group == 0:
                re, im = mid[a, base : base + 8, :], mid[a, base + 8 : base + 16, :]
            else:
                re = mid[a, base + 16 : base + 24, :]
                im = pair(re, 1)
            return re * c - im * s, im * c + re * s

        return load

    def last_chunk(a, _):
        for group in range(2):
            count = 8 if group == 0 else 4
            for n1, (re, im) in enumerate(dft32(untwist(sec_mid, a, group), 1)):
                sec_time[0, n1] = re
                sec_time[1, n1] = im
            for n1, (re, im) in enumerate(dft32(untwist(ref_mid, a, group), 1)):
                sr = sec_time[0, n1] * (1.0 / 1024)
                si = sec_time[1, n1] * (1.0 / 1024)
                at = group * 8 * 192 + (n1 * 3 + a) * 2
                out_ref[pl.ds(at, count, stride=192), :] = (sr * re + si * im)[0:count]
                out_ref[pl.ds(at + 1, count, stride=192), :] = (si * re - sr * im)[0:count]
        return 0

    lax.fori_loop(0, 3, last_chunk, 0)


def final(sec_blocks, lines, trig, inverse, project):
    return pl.pallas_call(
        final_kernel,
        out_shape=jax.ShapeDtypeStruct((2 * LINES * 96, 128), F32),
        scratch_shapes=[
            pltpu.VMEM((3, PEERS * ROWS, 128), F32),
            pltpu.VMEM((3, PEERS * ROWS, 128), F32),
            pltpu.VMEM((2, OUTER, 8, 128), F32),
        ],
        compiler_params=pltpu.CompilerParams(vmem_limit_bytes=VMEM_LIMIT),
        name="range_final",
    )(sec_blocks, lines, trig, inverse, project)


def body(reference_slc, secondary_slc, range_start, azimuth_start):
    own, full = azimuth_tables()
    basis, inverse, project = range_tables()
    trig = trig_values(range_start[0], azimuth_start[0], lax.axis_index("line"))
    sec = secondary_slc.reshape(2, LINES, 96, 128).transpose(1, 2, 0, 3).reshape(2 * LINES * 96, 128)
    ref = reference_slc.reshape(2, LINES, 6, 128).transpose(1, 2, 0, 3).reshape(2 * LINES * 6, 128)
    returned, lines = exchange(sec, ref, trig, jnp.asarray(basis), jnp.asarray(own), jnp.asarray(full))
    lines = lines.reshape(96, ROWS, 128)
    out = final(returned, lines, trig, jnp.asarray(inverse), jnp.asarray(project))
    return out.reshape(LINES, 96, 2, 128).transpose(2, 0, 1, 3).reshape(1, 2, LINES, RG)


def solution(mesh):
    in_specs = (P(None, "line", "date"), P("date", None, "line", None), P("date"), P("date"))
    out_specs = P("date", None, "line", None)
    return jax.shard_map(body, mesh=mesh, in_specs=in_specs, out_specs=out_specs, check_vma=False)
```

```python
import math

import jax
import jax.numpy as jnp
import ml_dtypes
import numpy as np
from jax import lax
from jax.experimental import pallas as pl
from jax.experimental.pallas import tpu as pltpu
from jax.sharding import PartitionSpec as P

RG = 12288
AZ = 384
OUTER = 32
INNER = 384
KEEP = 256
LINES = 12
ROWS = 24
PEERS = 32
MESH = pl.DeviceIdType.MESH
F32 = jnp.float32
BF16 = jnp.bfloat16
VMEM_LIMIT = 56 * 1024 * 1024


def row_line():
    return np.array(list(range(8)) + list(range(8)) + list(range(8, 12)) * 2)


def row_part():
    return np.array([0] * 8 + [1] * 8 + [0] * 4 + [1] * 4)


def dirichlet(offset, width, length):
    offset = np.asarray(offset)
    safe = np.where(offset == 0, 1, offset)
    value = np.sin(np.pi * width * safe / length) / (length * np.sin(np.pi * safe / length))
    return np.where(offset == 0, width / length, value)


def split_table(table):
    table = np.asarray(table, np.float32)
    high = table.astype(ml_dtypes.bfloat16)
    low = (table - high.astype(np.float32)).astype(ml_dtypes.bfloat16)
    return np.stack([high, low])


def azimuth_tables():
    lines = (np.arange(PEERS)[:, None] * LINES + row_line()[None]).reshape(-1)
    part = np.tile(row_part(), PEERS)
    full = dirichlet(lines[:, None] - lines[None, :], AZ // 2, AZ)
    own = full * (part[:, None] == part[None, :])
    return split_table(own), full.astype(np.float32).reshape(4, 192, 768)


def range_tables():
    n2 = np.arange(INNER)
    angle = 2 * np.pi * (np.arange(KEEP // 2)[None, :] + 0.5) * n2[:, None] / INNER
    basis = math.sqrt(2 / INNER) * np.concatenate([np.cos(angle), np.sin(angle)], 1)
    projection = dirichlet(n2[:, None] - n2[None, :], KEEP, INNER)
    return split_table(basis), split_table(basis.T / OUTER**2), split_table(projection)


def cmul_const(re, im, angle):
    c, s = math.cos(angle), math.sin(angle)
    if abs(c - 1) < 1e-12:
        return re, im
    if abs(c) < 1e-12:
        return (-im, re) if s > 0 else (im, -re)
    if abs(abs(c) - abs(s)) < 1e-12:
        r = math.sqrt(0.5)
        if c > 0 and s > 0:
            return (re - im) * r, (re + im) * r
        if c > 0:
            return (re + im) * r, (im - re) * r
        if s > 0:
            return (re + im) * -r, (re - im) * r
        return (im - re) * r, (re + im) * -r
    return re * c - im * s, re * s + im * c


def dft_small(values, sign):
    n = len(values)
    if n == 1:
        return values
    even = dft_small(values[0::2], sign)
    odd = dft_small(values[1::2], sign)
    low, high = [], []
    for k in range(n // 2):
        tr, ti = cmul_const(odd[k][0], odd[k][1], sign * 2 * math.pi * k / n)
        low.append((even[k][0] + tr, even[k][1] + ti))
        high.append((even[k][0] - tr, even[k][1] - ti))
    return low + high


def dft32(load, sign):
    middle = []
    for q in range(8):
        part = dft_small([load(q + 8 * p) for p in range(4)], sign)
        middle.append([cmul_const(*part[s], sign * 2 * math.pi * q * s / 32) for s in range(4)])
    out = [None] * 32
    for s in range(4):
        part = dft_small([middle[q][s] for q in range(8)], sign)
        for t in range(8):
            out[s + 4 * t] = part[t]
    return out


def split_value(x):
    high = x.astype(BF16)
    low = (x - high.astype(F32)).astype(BF16)
    return high, low


def dot(a, b):
    return jnp.dot(a, b, preferred_element_type=F32)


def dot3(a, b):
    return dot(a[0], b[0]) + dot(a[1], b[0]) + dot(a[0], b[1])


TWIST, VECTOR, PHASE, TRIG = 0, 192, 208, 240


def vector_table():
    table = np.zeros((2, 16, 128), np.float32)
    lines = (np.arange(PEERS)[:, None] * LINES + row_line()[None]).reshape(6, 128)
    real = np.tile(row_part() == 0, PEERS).reshape(6, 128)
    table[0, 0:6] = lines
    table[0, 8:14] = lines
    table[1, 0:6] = np.where(real, 0, -RG // 4)
    table[1, 8:14] = np.where(real, RG // 4, 0)
    return table


def cosine(turns):
    rest = turns - jnp.floor(turns * (1.0 / RG)) * RG
    half = (rest * (1.0 / RG) - 0.5) * math.pi
    square = half * half
    value = jnp.full_like(square, -1.0 / math.factorial(14))
    for k in range(6, -1, -1):
        value = value * square + (-1) ** k / math.factorial(2 * k)
    return 1 - 2 * value * value


def fill_trig(trig_ref, vector_ref, range_first, azimuth_first, line):
    k1 = lax.broadcasted_iota(jnp.int32, (OUTER, 128), 0)
    lane = lax.broadcasted_iota(jnp.int32, (OUTER, 128), 1)
    bins = (range_first + ((k1 - range_first) & (OUTER - 1)) + OUTER * (KEEP - 1) // 2).astype(F32)
    for a in range(3):
        turns = bins * (lane + a * 128).astype(F32)
        trig_ref[a * OUTER : (a + 1) * OUTER, :] = cosine(turns)
        trig_ref[96 + a * OUTER : 96 + (a + 1) * OUTER, :] = cosine(turns - RG // 4)
    factor = ((RG // (2 * AZ)) * (2 * azimuth_first + AZ // 2 - 1)).astype(F32)
    trig_ref[VECTOR : VECTOR + 16, :] = cosine(vector_ref[0] * factor + vector_ref[1])
    turns = (line * LINES + k1[0:16]).astype(F32) * factor
    trig_ref[PHASE : PHASE + 16, :] = cosine(turns)
    trig_ref[PHASE + 16 : PHASE + 32, :] = cosine(turns - RG // 4)


def remote(src, dst, send, recv, date, line):
    return pltpu.make_async_remote_copy(
        src_ref=src, dst_ref=dst, send_sem=send, recv_sem=recv, device_id=(date, line), device_id_type=MESH
    )


def chunk_of(zh, y):
    skip = 3 - y
    return jnp.where(zh > skip, zh - 1, zh), zh != skip


def get_pair(ref, base, group):
    if group == 0:
        return ref[base : base + 8, :], ref[base + 8 : base + 16, :]
    tile = ref[base + 16 : base + 24, :]
    return tile, pltpu.roll(tile, 4, 0)


def put_pair(ref, base, group, re, im):
    if group == 0:
        ref[base : base + 8, :] = re
        ref[base + 8 : base + 16, :] = im
    else:
        ref[base + 16 : base + 24, :] = jnp.concatenate([re[0:4], im[0:4]], 0)


def untwist(mid, trig_ref, a, group):
    def load(k1):
        c, s = twiddle(trig_ref, a, k1)
        re, im = get_pair(mid.at[a], k1 * ROWS, group)
        return re * c - im * s, im * c + re * s

    return load


def twiddle(trig_ref, a, k1):
    row = a * OUTER + k1
    return trig_ref[pl.ds(row, 1), :], trig_ref[pl.ds(96 + row, 1), :]


STEPS = 8
SECOND_AT = 5


def exchange_kernel(
    sec_ref, refr_ref, range_ref, azimuth_ref, vector_ref, basis_ref, inverse_ref, own_hbm, full_hbm,
    time_ref, lines_ref, trig_out,
    trig_ref, mid_ref, coef_ref, spread_ref, chunks_ref, all_ref, vecs_ref, filt_ref, back_ref, rout_ref,
    own_ref, full_ref, mixed_ref,
    a_send, a_recv, b_send, b_recv, x_send, x_recv, v_send, v_recv, y_send, y_recv,
    r_send, r_recv, l_send, l_recv, own_sem, xo_sem,
):
    d, l = lax.axis_index("date"), lax.axis_index("line")
    x, zh = d // 4, d % 4
    zl, u = l // 8, l % 8
    y = u // 2
    z = zh * 4 + zl
    up, down = (z + 1) % 16, (z + 15) % 16
    right = (x * 4 + up // 4, (up % 4) * 8 + u)
    left = (x * 4 + down // 4, (down % 4) * 8 + u)
    place = x * 8 + u
    mine, valid = chunk_of(zh, y)

    own_copy = pltpu.make_async_copy(own_hbm, own_ref, own_sem.at[4])
    own_copy.start()
    full_copy = pltpu.make_async_copy(full_hbm.at[zl], full_ref, own_sem.at[5])
    full_copy.start()

    def plane(i):
        other = (place + i) % PEERS
        ox, ou = other // 8, other % 8
        return other, ox, ou, ox * 4 + zh, zl * 8 + ou

    barrier = pltpu.get_barrier_semaphore()

    def greet(i, _):
        pl.semaphore_signal(barrier, inc=1, device_id=(d, (l + i) % PEERS), device_id_type=MESH)
        _, _, _, od, ol = plane(i)
        pl.semaphore_signal(barrier, inc=1, device_id=(od, ol), device_id_type=MESH)
        return 0

    pl.semaphore_signal(barrier, inc=1, device_id=right, device_id_type=MESH)
    pl.semaphore_signal(barrier, inc=1, device_id=left, device_id_type=MESH)
    lax.fori_loop(1, PEERS, greet, 0)

    for i in range(LINES):
        for part in range(2):
            row = i + 8 * part if i < 8 else 8 + i + 4 * part
            for c in range(6):
                chunks_ref[c, row : row + 1, :] = refr_ref[i, part : part + 1, c * 128 : (c + 1) * 128]

    fill_trig(trig_ref, vector_ref, range_ref[0], azimuth_ref[0], l)
    trig_out[...] = trig_ref[...]

    pl.semaphore_wait(barrier, 2 * (PEERS - 1) + 2)

    def y_slot(i, source):
        return all_ref.at[i, zl, pl.ds(pl.multiple_of(source * ROWS, 8), ROWS)]

    def y_copy(c):
        q = 6 * zh + c
        return remote(chunks_ref.at[c], y_slot(q // 8, u), y_send.at[c], y_recv.at[u], d, zl * 8 + q % 8)

    def y_own(c):
        return pltpu.make_async_copy(chunks_ref.at[c], y_slot((6 * zh + c) // 8, u), own_sem.at[0])

    for c in range(6):
        owner = (6 * zh + c) % 8

        @pl.when(owner != u)
        def _():
            y_copy(c).start()

        @pl.when(owner == u)
        def _():
            y_own(c).start()

    def v_copy(i, slot):
        return remote(
            trig_ref.at[pl.ds(VECTOR, 16)], vecs_ref.at[slot], v_send.at[i], v_recv.at[slot],
            (x + i) % 4 * 4 + zh, l,
        )

    for i in range(1, 4):
        v_copy(i, x).start()
    own_vec = pltpu.make_async_copy(trig_ref.at[pl.ds(VECTOR, 16)], vecs_ref.at[x], own_sem.at[1])
    own_vec.start()

    def chunk(a, _):
        for group in range(2):
            rows = 8 if group == 0 else 4
            first = 8 * group
            pc = trig_ref[PHASE + first : PHASE + first + rows, :]
            ps = trig_ref[PHASE + 16 + first : PHASE + 16 + first + rows, :]

            def load(n1):
                at = first * 192 + (n1 * 3 + a) * 2
                return sec_ref[pl.ds(at, rows, stride=192), :], sec_ref[pl.ds(at + 1, rows, stride=192), :]

            for k1, (re, im) in enumerate(dft32(load, -1)):
                c, s = twiddle(trig_ref, a, k1)
                re, im = re * c + im * s, im * c - re * s
                re, im = re * pc + im * ps, im * pc - re * ps
                put_pair(mid_ref.at[a], k1 * ROWS, group, re, im)
        return 0

    def ring_copy(origin, send, recv, step, to):
        i, ok = chunk_of(origin // 4, y)
        ref = all_ref.at[jnp.where(ok, i, 0), origin % 4]
        return ok, remote(ref, ref, send.at[step], recv.at[step], *to)

    def ring_start(s):
        ok, copy = ring_copy((z + 17 - s) % 16, r_send, r_recv, s, right)
        pl.when(ok)(copy.start)
        if s < STEPS:
            ok2, copy2 = ring_copy((z + s - 1) % 16, l_send, l_recv, s, left)
            pl.when(ok2)(copy2.start)

    def ring_sent(s):
        ok, copy = ring_copy((z + 17 - s) % 16, r_send, r_recv, s, right)
        pl.when(ok)(copy.wait_send)
        if s < STEPS:
            ok2, copy2 = ring_copy((z + s - 1) % 16, l_send, l_recv, s, left)
            pl.when(ok2)(copy2.wait_send)

    def ring_arrived(s):
        ok, copy = ring_copy((z + 16 - s) % 16, r_send, r_recv, s, left)
        pl.when(ok)(copy.wait_recv)
        if s < STEPS:
            ok2, copy2 = ring_copy((z + s) % 16, l_send, l_recv, s, right)
            pl.when(ok2)(copy2.wait_recv)

    def a_copy(to):
        return remote(coef_ref.at[to], spread_ref.at[l], a_send.at[to], a_recv.at[l], d, to)

    def send_blocks(copy, step):
        def send(i, _):
            to = step * 8 + (u + i) % 8
            pl.when(to != l)(copy(to).start)
            return 0

        lax.fori_loop(0, 8, send, 0)

    def rows(k, _):
        step = (zl + 1 + k) % 4
        at = pl.ds(pl.multiple_of(step * 192, 192), 192)
        block = jnp.concatenate([mid_ref[a, at, :] for a in range(3)], 1)
        result = dot3(split_value(block), (basis_ref[0], basis_ref[1]))
        coef_ref[pl.ds(step * 8, 8)] = result.reshape(8, ROWS, KEEP)
        send_blocks(a_copy, step)
        return 0

    def a_own():
        return pltpu.make_async_copy(coef_ref.at[l], spread_ref.at[l], own_sem.at[2])

    def mix():
        row = lax.broadcasted_iota(jnp.int32, (ROWS, 128), 0)
        real = (row < 8) | ((row >= 16) & (row < 20))
        for i in range(1, 4):
            v_copy(i, (x + i) % 4).wait_recv()
        own_vec.wait()
        full_copy.wait()

        def date(t, _):
            at = pl.ds(pl.multiple_of(t * 8 * ROWS, 8 * ROWS), 8 * ROWS)
            for j in range(6):
                lanes = slice(j * 128, (j + 1) * 128)
                mixed = jnp.where(real, vecs_ref[t, j : j + 1, :], vecs_ref[t, 8 + j : 9 + j, :])
                part = (full_ref[:, lanes].reshape(8, ROWS, 128) * mixed[None]).reshape(8 * ROWS, 128)
                high, low = split_value(part)
                mixed_ref[0, at, lanes] = high
                mixed_ref[1, at, lanes] = low
            return 0

        lax.fori_loop(0, 4, date, 0)

    def x_copy(t, i, ou):
        return remote(
            rout_ref.at[t, i, ou], lines_ref.at[x, i, u], x_send.at[(t * 3 + i) * 8 + ou],
            x_recv.at[i * PEERS + place], t * 4 + zh, zl * 8 + ou,
        )

    def x_own(i):
        return pltpu.make_async_copy(rout_ref.at[x, i, u], lines_ref.at[x, i, u], xo_sem.at[i])

    def ref_chunk(block):
        i, ok = chunk_of(block % 4, y)

        @pl.when(ok)
        def _():
            samples = split_value(all_ref[i].reshape(2 * AZ, 128))

            def date(k, _):
                t = (x + 1 + k) % 4
                at = pl.ds(pl.multiple_of(t * 8 * ROWS, 8 * ROWS), 8 * ROWS)
                result = dot3((mixed_ref[0, at, :], mixed_ref[1, at, :]), samples)
                rout_ref[t, i] = result.reshape(8, ROWS, 128)

                def send(j, _):
                    ou = (u + j) % 8
                    pl.when((t != x) | (ou != u))(x_copy(t, i, ou).start)
                    return 0

                lax.fori_loop(0, 8, send, 0)
                return 0

            lax.fori_loop(0, 4, date, 0)
            x_own(i).start()

    def b_copy(to):
        return remote(filt_ref.at[to], back_ref.at[l], b_send.at[to], b_recv.at[l], d, to)

    def b_own():
        return pltpu.make_async_copy(filt_ref.at[l], back_ref.at[l], own_sem.at[3])

    def second():
        a_own().wait()
        own_copy.wait()

        def arrived(i, _):
            source = (l + i) % PEERS
            remote(
                coef_ref.at[source], spread_ref.at[source], a_send.at[source], a_recv.at[source], d, source
            ).wait_recv()
            return 0

        lax.fori_loop(1, PEERS, arrived, 0)
        sec = split_value(spread_ref[...].reshape(PEERS * ROWS, KEEP))

        def sec_rows(k, _):
            step = (zl + 1 + k) % 4
            at = pl.ds(pl.multiple_of(step * 192, 192), 192)
            result = dot3((own_ref[0, at, :], own_ref[1, at, :]), sec)
            filt_ref[pl.ds(step * 8, 8)] = result.reshape(8, ROWS, KEEP)
            send_blocks(b_copy, step)
            return 0

        lax.fori_loop(0, 4, sec_rows, 0)
        b_own().start()

    def inverse():
        b_own().wait()

        def arrived(i, _):
            source = (l + i) % PEERS
            remote(
                filt_ref.at[source], back_ref.at[source], b_send.at[source], b_recv.at[source], d, source
            ).wait_recv()
            return 0

        lax.fori_loop(1, PEERS, arrived, 0)

        def inverse_rows(step, _):
            at = pl.ds(pl.multiple_of(step * 192, 192), 192)
            block = split_value(back_ref[pl.ds(step * 8, 8)].reshape(192, KEEP))
            result = dot3(block, (inverse_ref[0], inverse_ref[1]))
            for a in range(3):
                mid_ref[a, at, :] = result[:, a * 128 : (a + 1) * 128]
            return 0

        lax.fori_loop(0, 4, inverse_rows, 0)

        def time_chunk(a, _):
            for group in range(2):
                for n1, (re, im) in enumerate(dft32(untwist(mid_ref, trig_ref, a, group), 1)):
                    put_pair(time_ref.at[n1 * 3 + a], 0, group, re, im)
            return 0

        lax.fori_loop(0, 3, time_chunk, 0)

    chunk(0, 0)

    @pl.when(valid)
    def _():
        for i in range(1, 8):
            source = (u + i) % 8
            remote(
                chunks_ref.at[0], y_slot(mine, source), y_send.at[0], y_recv.at[source], d, zl * 8 + source
            ).wait_recv()
        y_own(0).wait()

    ring_start(1)
    lax.fori_loop(1, 3, chunk, 0)
    ring_arrived(1)
    ring_start(2)
    lax.fori_loop(0, 4, rows, 0)
    a_own().start()
    mix()
    for s in range(2, STEPS + 1):
        ring_arrived(s)
        if s < STEPS:
            ring_start(s + 1)
        if s == 3:
            ref_chunk(zh)
        if s == SECOND_AT:
            second()
        if s == STEPS - 1:
            ref_chunk(zh + 1)
            ref_chunk(zh + 3)
    ref_chunk(zh + 2)
    inverse()

    for s in range(1, STEPS + 1):
        ring_sent(s)
    for i in range(1, 4):
        v_copy(i, x).wait_send()
    for c in range(6):
        owner = (6 * zh + c) % 8

        @pl.when(owner != u)
        def _():
            y_copy(c).wait_send()

    def finish(k, _):
        other, ox, ou, od, ol = plane(k)
        for i in range(3):
            copy = remote(
                rout_ref.at[ox, i, ou], lines_ref.at[ox, i, ou], x_send.at[(ox * 3 + i) * 8 + ou],
                x_recv.at[i * PEERS + other], od, ol,
            )
            copy.wait_send()
            copy.wait_recv()
        to = (l + k) % PEERS
        a_copy(to).wait_send()
        b_copy(to).wait_send()
        return 0

    for i in range(3):
        x_own(i).wait()
    lax.fori_loop(1, PEERS, finish, 0)


def exchange(sec, ref, range_start, azimuth_start, vector, basis, inverse, own, full):
    any_space = pl.BlockSpec(memory_space=pl.ANY)
    vmem = pl.BlockSpec(memory_space=pltpu.VMEM)
    smem = pl.BlockSpec(memory_space=pltpu.SMEM)
    dma = pltpu.SemaphoreType.DMA
    blocks = (PEERS, ROWS, KEEP)
    lines = (4, 3, 8, ROWS, 128)
    peers = dma((PEERS,))
    ring = dma((STEPS + 1,))
    return pl.pallas_call(
        exchange_kernel,
        out_shape=(
            jax.ShapeDtypeStruct((96, ROWS, 128), F32),
            jax.ShapeDtypeStruct(lines, F32),
            jax.ShapeDtypeStruct((TRIG, 128), F32),
        ),
        in_specs=[vmem, vmem, smem, smem, vmem, vmem, vmem, any_space, any_space],
        out_specs=(vmem, any_space, vmem),
        scratch_shapes=[
            pltpu.VMEM((TRIG, 128), F32),
            pltpu.VMEM((3, PEERS * ROWS, 128), F32),
            pltpu.VMEM(blocks, F32),
            pltpu.VMEM(blocks, F32),
            pltpu.VMEM((6, ROWS, 128), F32),
            pltpu.VMEM((3, 4, 8 * ROWS, 128), F32),
            pltpu.VMEM((4, 16, 128), F32),
            pltpu.VMEM(blocks, F32),
            pltpu.VMEM(blocks, F32),
            pltpu.VMEM(lines, F32),
            pltpu.VMEM((2, 2 * AZ, 2 * AZ), BF16),
            pltpu.VMEM((8 * ROWS, 2 * AZ), F32),
            pltpu.VMEM((2, 2 * AZ, 2 * AZ), BF16),
            peers, peers, peers, peers, dma((3 * PEERS,)), dma((3 * PEERS,)),
            dma((4,)), dma((4,)), dma((6,)), dma((8,)),
            ring, ring, ring, ring, dma((6,)), dma((3,)),
        ],
        compiler_params=pltpu.CompilerParams(
            collective_id=1, has_side_effects=True, vmem_limit_bytes=VMEM_LIMIT
        ),
        name="exchange",
    )(sec, ref, range_start, azimuth_start, vector, basis, inverse, own, full)


def final_kernel(time_ref, lines_ref, trig_ref, project_ref, out_ref, mid_ref):
    def forward_chunk(a, _):
        for group in range(2):

            def load(n1):
                return get_pair(lines_ref.at[n1 * 3 + a], 0, group)

            for k1, (re, im) in enumerate(dft32(load, -1)):
                c, s = twiddle(trig_ref, a, k1)
                put_pair(mid_ref.at[a], k1 * ROWS, group, re * c + im * s, im * c - re * s)
        return 0

    lax.fori_loop(0, 3, forward_chunk, 0)

    def rows(step, _):
        at = pl.ds(pl.multiple_of(step * 192, 192), 192)
        block = jnp.concatenate([mid_ref[a, at, :] for a in range(3)], 1)
        result = dot3(split_value(block), (project_ref[0], project_ref[1]))
        for a in range(3):
            mid_ref[a, at, :] = result[:, a * 128 : (a + 1) * 128]
        return 0

    lax.fori_loop(0, 4, rows, 0)

    def last_chunk(a, _):
        for group in range(2):
            count = 8 if group == 0 else 4
            for n1, (re, im) in enumerate(dft32(untwist(mid_ref, trig_ref, a, group), 1)):
                sr, si = get_pair(time_ref.at[n1 * 3 + a], 0, group)
                at = group * 8 * 192 + (n1 * 3 + a) * 2
                out_ref[pl.ds(at, count, stride=192), :] = (sr * re + si * im)[0:count]
                out_ref[pl.ds(at + 1, count, stride=192), :] = (si * re - sr * im)[0:count]
        return 0

    lax.fori_loop(0, 3, last_chunk, 0)


def final(time, lines, trig, project):
    return pl.pallas_call(
        final_kernel,
        out_shape=jax.ShapeDtypeStruct((2 * LINES * 96, 128), F32),
        scratch_shapes=[pltpu.VMEM((3, PEERS * ROWS, 128), F32)],
        compiler_params=pltpu.CompilerParams(vmem_limit_bytes=VMEM_LIMIT),
        name="range_final",
    )(time, lines, trig, project)


def body(reference_slc, secondary_slc, range_start, azimuth_start):
    own, full = (jnp.asarray(t) for t in azimuth_tables())
    basis, inverse, project = (jnp.asarray(t) for t in range_tables())
    sec = secondary_slc.reshape(2, LINES, 96, 128).transpose(1, 2, 0, 3).reshape(2 * LINES * 96, 128)
    ref = reference_slc.transpose(1, 0, 2)
    time, lines, trig = exchange(
        sec, ref, range_start, azimuth_start, jnp.asarray(vector_table()), basis, inverse, own, full
    )
    out = final(time, lines.reshape(96, ROWS, 128), trig, project)
    return out.reshape(LINES, 96, 2, 128).transpose(2, 0, 1, 3).reshape(1, 2, LINES, RG)


def solution(mesh):
    in_specs = (P(None, "line", "date"), P("date", None, "line", None), P("date"), P("date"))
    out_specs = P("date", None, "line", None)
    return jax.shard_map(body, mesh=mesh, in_specs=in_specs, out_specs=out_specs, check_vma=False)
```

```python
import math

import jax
import jax.numpy as jnp
import ml_dtypes
import numpy as np
from jax import lax
from jax.experimental import pallas as pl
from jax.experimental.pallas import tpu as pltpu
from jax.sharding import PartitionSpec as P

RG = 12288
AZ = 384
OUTER = 32
INNER = 384
KEEP = 256
LINES = 12
ROWS = 24
PEERS = 32
MESH = pl.DeviceIdType.MESH
F32 = jnp.float32
BF16 = jnp.bfloat16
VMEM_LIMIT = 56 * 1024 * 1024


def row_line():
    return np.array(list(range(8)) + list(range(8)) + list(range(8, 12)) * 2)


def row_part():
    return np.array([0] * 8 + [1] * 8 + [0] * 4 + [1] * 4)


def dirichlet(offset, width, length):
    offset = np.asarray(offset)
    safe = np.where(offset == 0, 1, offset)
    value = np.sin(np.pi * width * safe / length) / (length * np.sin(np.pi * safe / length))
    return np.where(offset == 0, width / length, value)


def split_table(table):
    table = np.asarray(table, np.float32)
    high = table.astype(ml_dtypes.bfloat16)
    low = (table - high.astype(np.float32)).astype(ml_dtypes.bfloat16)
    return np.stack([high, low])


def azimuth_tables():
    lines = (np.arange(PEERS)[:, None] * LINES + row_line()[None]).reshape(-1)
    part = np.tile(row_part(), PEERS)
    full = dirichlet(lines[:, None] - lines[None, :], AZ // 2, AZ)
    own = full * (part[:, None] == part[None, :])
    return split_table(own), full.astype(np.float32).reshape(4, 192, 768)


def range_tables():
    n2 = np.arange(INNER)
    angle = 2 * np.pi * (np.arange(KEEP // 2)[None, :] + 0.5) * n2[:, None] / INNER
    basis = math.sqrt(2 / INNER) * np.concatenate([np.cos(angle), np.sin(angle)], 1)
    projection = dirichlet(n2[:, None] - n2[None, :], KEEP, INNER)
    return split_table(basis), split_table(basis.T / OUTER**2), split_table(projection)


def cmul_const(re, im, angle):
    c, s = math.cos(angle), math.sin(angle)
    if abs(c - 1) < 1e-12:
        return re, im
    if abs(c) < 1e-12:
        return (-im, re) if s > 0 else (im, -re)
    if abs(abs(c) - abs(s)) < 1e-12:
        r = math.sqrt(0.5)
        if c > 0 and s > 0:
            return (re - im) * r, (re + im) * r
        if c > 0:
            return (re + im) * r, (im - re) * r
        if s > 0:
            return (re + im) * -r, (re - im) * r
        return (im - re) * r, (re + im) * -r
    return re * c - im * s, re * s + im * c


def dft_small(values, sign):
    n = len(values)
    if n == 1:
        return values
    even = dft_small(values[0::2], sign)
    odd = dft_small(values[1::2], sign)
    low, high = [], []
    for k in range(n // 2):
        tr, ti = cmul_const(odd[k][0], odd[k][1], sign * 2 * math.pi * k / n)
        low.append((even[k][0] + tr, even[k][1] + ti))
        high.append((even[k][0] - tr, even[k][1] - ti))
    return low + high


def dft32(load, sign):
    middle = []
    for q in range(8):
        part = dft_small([load(q + 8 * p) for p in range(4)], sign)
        middle.append([cmul_const(*part[s], sign * 2 * math.pi * q * s / 32) for s in range(4)])
    out = [None] * 32
    for s in range(4):
        part = dft_small([middle[q][s] for q in range(8)], sign)
        for t in range(8):
            out[s + 4 * t] = part[t]
    return out


def split_value(x):
    high = x.astype(BF16)
    low = (x - high.astype(F32)).astype(BF16)
    return high, low


def dot(a, b):
    return jnp.dot(a, b, preferred_element_type=F32)


def dot3(a, b):
    return dot(a[0], b[0]) + dot(a[1], b[0]) + dot(a[0], b[1])


TWIST, VECTOR, PHASE, TRIG = 0, 192, 208, 240


def vector_table():
    table = np.zeros((2, 16, 128), np.float32)
    lines = (np.arange(PEERS)[:, None] * LINES + row_line()[None]).reshape(6, 128)
    real = np.tile(row_part() == 0, PEERS).reshape(6, 128)
    table[0, 0:6] = lines
    table[0, 8:14] = lines
    table[1, 0:6] = np.where(real, 0, -RG // 4)
    table[1, 8:14] = np.where(real, RG // 4, 0)
    return table


def cosine(turns):
    rest = turns - jnp.floor(turns * (1.0 / RG)) * RG
    half = (rest * (1.0 / RG) - 0.5) * math.pi
    square = half * half
    value = jnp.full_like(square, -1.0 / math.factorial(14))
    for k in range(6, -1, -1):
        value = value * square + (-1) ** k / math.factorial(2 * k)
    return 1 - 2 * value * value


def fill_trig(trig_ref, vector_ref, range_first, azimuth_first, line):
    k1 = lax.broadcasted_iota(jnp.int32, (OUTER, 128), 0)
    lane = lax.broadcasted_iota(jnp.int32, (OUTER, 128), 1)
    bins = (range_first + ((k1 - range_first) & (OUTER - 1)) + OUTER * (KEEP - 1) // 2).astype(F32)
    for a in range(3):
        turns = bins * (lane + a * 128).astype(F32)
        trig_ref[a * OUTER : (a + 1) * OUTER, :] = cosine(turns)
        trig_ref[96 + a * OUTER : 96 + (a + 1) * OUTER, :] = cosine(turns - RG // 4)
    factor = ((RG // (2 * AZ)) * (2 * azimuth_first + AZ // 2 - 1)).astype(F32)
    trig_ref[VECTOR : VECTOR + 16, :] = cosine(vector_ref[0] * factor + vector_ref[1])
    turns = (line * LINES + k1[0:16]).astype(F32) * factor
    trig_ref[PHASE : PHASE + 16, :] = cosine(turns)
    trig_ref[PHASE + 16 : PHASE + 32, :] = cosine(turns - RG // 4)


def remote(src, dst, send, recv, date, line):
    return pltpu.make_async_remote_copy(
        src_ref=src, dst_ref=dst, send_sem=send, recv_sem=recv, device_id=(date, line), device_id_type=MESH
    )


def chunk_of(zh, y):
    skip = 3 - y
    return jnp.where(zh > skip, zh - 1, zh), zh != skip


def get_pair(ref, base, group):
    if group == 0:
        return ref[base : base + 8, :], ref[base + 8 : base + 16, :]
    tile = ref[base + 16 : base + 24, :]
    return tile, pltpu.roll(tile, 4, 0)


def put_pair(ref, base, group, re, im):
    if group == 0:
        ref[base : base + 8, :] = re
        ref[base + 8 : base + 16, :] = im
    else:
        ref[base + 16 : base + 24, :] = jnp.concatenate([re[0:4], im[0:4]], 0)


def untwist(mid, trig_ref, a, group):
    def load(k1):
        c, s = twiddle(trig_ref, a, k1)
        re, im = get_pair(mid.at[a], k1 * ROWS, group)
        return re * c - im * s, im * c + re * s

    return load


def twiddle(trig_ref, a, k1):
    row = a * OUTER + k1
    return trig_ref[pl.ds(row, 1), :], trig_ref[pl.ds(96 + row, 1), :]


STEPS = 8
PIECES = 2
PIECE = 8 * ROWS // PIECES


def exchange_kernel(
    sec_ref, refr_ref, range_ref, azimuth_ref, vector_ref, basis_ref, project_ref, own_hbm, full_hbm,
    back_ref, time_out, trig_out,
    trig_ref, mid_ref, coef_ref, spread_ref, chunks_ref, all_ref, vecs_ref, filt_ref, lines_ref, time_ref, rout_ref,
    own_ref, full_ref, mixed_ref,
    a_send, a_recv, b_send, b_recv, x_send, x_recv, v_send, v_recv, y_send, y_recv,
    r_send, r_recv, l_send, l_recv, own_sem, xo_sem,
):
    d, l = lax.axis_index("date"), lax.axis_index("line")
    x, zh = d // 4, d % 4
    zl, u = l // 8, l % 8
    y = u // 2
    z = zh * 4 + zl
    up, down = (z + 1) % 16, (z + 15) % 16
    right = (x * 4 + up // 4, (up % 4) * 8 + u)
    left = (x * 4 + down // 4, (down % 4) * 8 + u)
    place = x * 8 + u
    mine, valid = chunk_of(zh, y)

    own_copy = pltpu.make_async_copy(own_hbm, own_ref, own_sem.at[4])
    own_copy.start()
    full_copy = pltpu.make_async_copy(full_hbm.at[zl], full_ref, own_sem.at[5])
    full_copy.start()

    def plane(i):
        other = (place + i) % PEERS
        ox, ou = other // 8, other % 8
        return other, ox, ou, ox * 4 + zh, zl * 8 + ou

    barrier = pltpu.get_barrier_semaphore()

    def greet(i, _):
        pl.semaphore_signal(barrier, inc=1, device_id=(d, (l + i) % PEERS), device_id_type=MESH)
        _, _, _, od, ol = plane(i)
        pl.semaphore_signal(barrier, inc=1, device_id=(od, ol), device_id_type=MESH)
        return 0

    pl.semaphore_signal(barrier, inc=1, device_id=right, device_id_type=MESH)
    pl.semaphore_signal(barrier, inc=1, device_id=left, device_id_type=MESH)
    lax.fori_loop(1, PEERS, greet, 0)

    for i in range(LINES):
        for part in range(2):
            row = i + 8 * part if i < 8 else 8 + i + 4 * part
            for c in range(6):
                chunks_ref[c, row : row + 1, :] = refr_ref[i, part : part + 1, c * 128 : (c + 1) * 128]

    fill_trig(trig_ref, vector_ref, range_ref[0], azimuth_ref[0], l)
    trig_out[...] = trig_ref[...]

    pl.semaphore_wait(barrier, 2 * (PEERS - 1) + 2)

    def y_slot(i, source):
        return all_ref.at[i, zl, pl.ds(pl.multiple_of(source * ROWS, 8), ROWS)]

    def y_copy(c):
        q = 6 * zh + c
        return remote(chunks_ref.at[c], y_slot(q // 8, u), y_send.at[c], y_recv.at[u], d, zl * 8 + q % 8)

    def y_own(c):
        return pltpu.make_async_copy(chunks_ref.at[c], y_slot((6 * zh + c) // 8, u), own_sem.at[0])

    for c in range(6):
        owner = (6 * zh + c) % 8

        @pl.when(owner != u)
        def _():
            y_copy(c).start()

        @pl.when(owner == u)
        def _():
            y_own(c).start()

    def v_copy(i, slot):
        return remote(
            trig_ref.at[pl.ds(VECTOR, 16)], vecs_ref.at[slot], v_send.at[i], v_recv.at[slot],
            (x + i) % 4 * 4 + zh, l,
        )

    for i in range(1, 4):
        v_copy(i, x).start()
    own_vec = pltpu.make_async_copy(trig_ref.at[pl.ds(VECTOR, 16)], vecs_ref.at[x], own_sem.at[1])
    own_vec.start()

    def chunk(a, _):
        for group in range(2):
            rows = 8 if group == 0 else 4
            first = 8 * group
            pc = trig_ref[PHASE + first : PHASE + first + rows, :]
            ps = trig_ref[PHASE + 16 + first : PHASE + 16 + first + rows, :]

            def load(n1):
                at = first * 192 + (n1 * 3 + a) * 2
                return sec_ref[pl.ds(at, rows, stride=192), :], sec_ref[pl.ds(at + 1, rows, stride=192), :]

            for k1, (re, im) in enumerate(dft32(load, -1)):
                c, s = twiddle(trig_ref, a, k1)
                re, im = re * c + im * s, im * c - re * s
                re, im = re * pc + im * ps, im * pc - re * ps
                put_pair(mid_ref.at[a], k1 * ROWS, group, re, im)
        return 0

    def ring_copy(origin, send, recv, step, piece, to):
        i, ok = chunk_of(origin // 4, y)
        ref = all_ref.at[jnp.where(ok, i, 0), origin % 4, pl.ds(piece * PIECE, PIECE)]
        at = step * PIECES + piece
        return ok, remote(ref, ref, send.at[at], recv.at[at], *to)

    def ring_start(s, p):
        ok, copy = ring_copy((z + 17 - s) % 16, r_send, r_recv, s, p, right)
        pl.when(ok)(copy.start)
        if s < STEPS:
            ok2, copy2 = ring_copy((z + s - 1) % 16, l_send, l_recv, s, p, left)
            pl.when(ok2)(copy2.start)

    def ring_sent(s, p):
        ok, copy = ring_copy((z + 17 - s) % 16, r_send, r_recv, s, p, right)
        pl.when(ok)(copy.wait_send)
        if s < STEPS:
            ok2, copy2 = ring_copy((z + s - 1) % 16, l_send, l_recv, s, p, left)
            pl.when(ok2)(copy2.wait_send)

    def ring_arrived(s, p):
        ok, copy = ring_copy((z + 16 - s) % 16, r_send, r_recv, s, p, left)
        pl.when(ok)(copy.wait_recv)
        if s < STEPS:
            ok2, copy2 = ring_copy((z + s) % 16, l_send, l_recv, s, p, right)
            pl.when(ok2)(copy2.wait_recv)

    def ring_step(s):
        for p in range(PIECES):
            if s > 1:
                ring_arrived(s - 1, p)
            if s <= STEPS:
                ring_start(s, p)

    def a_copy(to):
        return remote(coef_ref.at[to], spread_ref.at[l], a_send.at[to], a_recv.at[l], d, to)

    def send_blocks(copy, step):
        def send(i, _):
            to = step * 8 + (u + i) % 8
            pl.when(to != l)(copy(to).start)
            return 0

        lax.fori_loop(0, 8, send, 0)

    def rows(k, _):
        step = (zl + k) % 4
        at = pl.ds(pl.multiple_of(step * 192, 192), 192)
        block = jnp.concatenate([mid_ref[a, at, :] for a in range(3)], 1)
        result = dot3(split_value(block), (basis_ref[0], basis_ref[1]))
        coef_ref[pl.ds(step * 8, 8)] = result.reshape(8, ROWS, KEEP)
        return 0

    def cross(k, _):
        send_blocks(a_copy, (zl + k) % 4)
        return 0

    def cross_part(part):
        def send(n, _):
            copy = a_copy((zl + 1 + n // 8) % 4 * 8 + (u + n) % 8)
            copy.start()
            return 0

        lax.fori_loop(4 * part, 4 * part + 4, send, 0)

    def a_own():
        return pltpu.make_async_copy(coef_ref.at[l], spread_ref.at[l], own_sem.at[2])

    def mix():
        row = lax.broadcasted_iota(jnp.int32, (ROWS, 128), 0)
        real = (row < 8) | ((row >= 16) & (row < 20))
        for i in range(1, 4):
            v_copy(i, (x + i) % 4).wait_recv()
        own_vec.wait()
        full_copy.wait()

        def date(t, _):
            at = pl.ds(pl.multiple_of(t * 8 * ROWS, 8 * ROWS), 8 * ROWS)
            for j in range(6):
                lanes = slice(j * 128, (j + 1) * 128)
                mixed = jnp.where(real, vecs_ref[t, j : j + 1, :], vecs_ref[t, 8 + j : 9 + j, :])
                part = (full_ref[:, lanes].reshape(8, ROWS, 128) * mixed[None]).reshape(8 * ROWS, 128)
                high, low = split_value(part)
                mixed_ref[0, at, lanes] = high
                mixed_ref[1, at, lanes] = low
            return 0

        lax.fori_loop(0, 4, date, 0)

    def x_copy(t, i, ou):
        return remote(
            rout_ref.at[t, i, ou], lines_ref.at[x * 24 + i * 8 + u], x_send.at[(t * 3 + i) * 8 + ou],
            x_recv.at[i * PEERS + place], t * 4 + zh, zl * 8 + ou,
        )

    def x_own(i):
        return pltpu.make_async_copy(rout_ref.at[x, i, u], lines_ref.at[x * 24 + i * 8 + u], xo_sem.at[i])

    def ref_chunk(block):
        i, ok = chunk_of(block % 4, y)

        @pl.when(ok)
        def _():
            samples = split_value(all_ref[i].reshape(2 * AZ, 128))

            def date(k, _):
                t = (x + 1 + k) % 4
                at = pl.ds(pl.multiple_of(t * 8 * ROWS, 8 * ROWS), 8 * ROWS)
                result = dot3((mixed_ref[0, at, :], mixed_ref[1, at, :]), samples)
                rout_ref[t, i] = result.reshape(8, ROWS, 128)

                def send(j, _):
                    ou = (u + j) % 8
                    pl.when((t != x) | (ou != u))(x_copy(t, i, ou).start)
                    return 0

                lax.fori_loop(0, 8, send, 0)
                return 0

            lax.fori_loop(0, 4, date, 0)
            x_own(i).start()

    def b_copy(to):
        return remote(filt_ref.at[to], back_ref.at[l], b_send.at[to], b_recv.at[l], d, to)

    def b_own():
        return pltpu.make_async_copy(filt_ref.at[l], back_ref.at[l], own_sem.at[3])

    def second():
        a_own().wait()
        own_copy.wait()

        def arrived(i, _):
            source = (l + i) % PEERS
            remote(
                coef_ref.at[source], spread_ref.at[source], a_send.at[source], a_recv.at[source], d, source
            ).wait_recv()
            return 0

        lax.fori_loop(1, PEERS, arrived, 0)
        sec = split_value(spread_ref[...].reshape(PEERS * ROWS, KEEP))

        def sec_rows(k, _):
            step = (zl + 1 + k) % 4
            at = pl.ds(pl.multiple_of(step * 192, 192), 192)
            result = dot3((own_ref[0, at, :], own_ref[1, at, :]), sec)
            filt_ref[pl.ds(step * 8, 8)] = result.reshape(8, ROWS, KEEP)
            send_blocks(b_copy, step)
            return 0

        lax.fori_loop(0, 4, sec_rows, 0)
        b_own().start()

    def x_other(k, i):
        other, ox, ou, od, ol = plane(k)
        return remote(
            rout_ref.at[ox, i, ou], lines_ref.at[ox * 24 + i * 8 + ou], x_send.at[(ox * 3 + i) * 8 + ou],
            x_recv.at[i * PEERS + other], od, ol,
        )

    def time_copy():
        return pltpu.make_async_copy(time_ref, time_out, own_sem.at[1])

    def ref_range():
        def arrived(k, _):
            for i in range(3):
                x_other(k, i).wait_recv()
            return 0

        for i in range(3):
            x_own(i).wait()
        lax.fori_loop(1, PEERS, arrived, 0)

        def forward_chunk(a, _):
            for group in range(2):

                def load(n1):
                    return get_pair(lines_ref.at[n1 * 3 + a], 0, group)

                for k1, (re, im) in enumerate(dft32(load, -1)):
                    c, s = twiddle(trig_ref, a, k1)
                    put_pair(mid_ref.at[a], k1 * ROWS, group, re * c + im * s, im * c - re * s)
            return 0

        lax.fori_loop(0, 3, forward_chunk, 0)

        def project_rows(step, _):
            at = pl.ds(pl.multiple_of(step * 192, 192), 192)
            block = jnp.concatenate([mid_ref[a, at, :] for a in range(3)], 1)
            result = dot3(split_value(block), (project_ref[0], project_ref[1]))
            for a in range(3):
                mid_ref[a, at, :] = result[:, a * 128 : (a + 1) * 128]
            return 0

        lax.fori_loop(0, 4, project_rows, 0)

        def time_chunk(a, _):
            for group in range(2):
                for n1, (re, im) in enumerate(dft32(untwist(mid_ref, trig_ref, a, group), 1)):
                    put_pair(time_ref.at[n1 * 3 + a], 0, group, re, im)
            return 0

        lax.fori_loop(0, 3, time_chunk, 0)
        time_copy().start()

    chunk(0, 0)

    @pl.when(valid)
    def _():
        for i in range(1, 8):
            source = (u + i) % 8
            remote(
                chunks_ref.at[0], y_slot(mine, source), y_send.at[0], y_recv.at[source], d, zl * 8 + source
            ).wait_recv()
        y_own(0).wait()

    ring_step(1)
    lax.fori_loop(1, 3, chunk, 0)
    ring_step(2)
    lax.fori_loop(0, 4, rows, 0)
    a_own().start()
    cross(0, 0)
    mix()
    for s in range(3, STEPS + 1):
        ring_step(s)
        if s - 3 < 6:
            cross_part(s - 3)
        if s == 4:
            ref_chunk(zh)
        if s == 99:
            second()
    ref_chunk(zh + 1)
    ref_chunk(zh + 3)
    second()
    ring_step(STEPS + 1)
    ref_chunk(zh + 2)
    ref_range()
    for s in range(1, STEPS + 1):
        for p in range(PIECES):
            ring_sent(s, p)
    for i in range(1, 4):
        v_copy(i, x).wait_send()
    for c in range(6):
        owner = (6 * zh + c) % 8

        @pl.when(owner != u)
        def _():
            y_copy(c).wait_send()

    def finish(k, _):
        for i in range(3):
            x_other(k, i).wait_send()
        to = (l + k) % PEERS
        a_copy(to).wait_send()
        b_copy(to).wait_send()
        remote(filt_ref.at[to], back_ref.at[to], b_send.at[to], b_recv.at[to], d, to).wait_recv()
        return 0

    lax.fori_loop(1, PEERS, finish, 0)
    b_own().wait()
    time_copy().wait()


def exchange(sec, ref, range_start, azimuth_start, vector, basis, project, own, full):
    any_space = pl.BlockSpec(memory_space=pl.ANY)
    vmem = pl.BlockSpec(memory_space=pltpu.VMEM)
    smem = pl.BlockSpec(memory_space=pltpu.SMEM)
    dma = pltpu.SemaphoreType.DMA
    blocks = (PEERS, ROWS, KEEP)
    time = (96, ROWS, 128)
    peers = dma((PEERS,))
    ring = dma(((STEPS + 1) * PIECES,))
    return pl.pallas_call(
        exchange_kernel,
        out_shape=(
            jax.ShapeDtypeStruct(blocks, F32),
            jax.ShapeDtypeStruct(time, F32),
            jax.ShapeDtypeStruct((TRIG, 128), F32),
        ),
        in_specs=[vmem, vmem, smem, smem, vmem, vmem, vmem, any_space, any_space],
        out_specs=(any_space, any_space, vmem),
        scratch_shapes=[
            pltpu.VMEM((TRIG, 128), F32),
            pltpu.VMEM((3, PEERS * ROWS, 128), F32),
            pltpu.VMEM(blocks, F32),
            pltpu.VMEM(blocks, F32),
            pltpu.VMEM((6, ROWS, 128), F32),
            pltpu.VMEM((3, 4, 8 * ROWS, 128), F32),
            pltpu.VMEM((4, 16, 128), F32),
            pltpu.VMEM(blocks, F32),
            pltpu.VMEM(time, F32),
            pltpu.VMEM(time, F32),
            pltpu.VMEM((4, 3, 8, ROWS, 128), F32),
            pltpu.VMEM((2, 2 * AZ, 2 * AZ), BF16),
            pltpu.VMEM((8 * ROWS, 2 * AZ), F32),
            pltpu.VMEM((2, 2 * AZ, 2 * AZ), BF16),
            peers, peers, peers, peers, dma((3 * PEERS,)), dma((3 * PEERS,)),
            dma((4,)), dma((4,)), dma((6,)), dma((8,)),
            ring, ring, ring, ring, dma((6,)), dma((3,)),
        ],
        compiler_params=pltpu.CompilerParams(
            collective_id=1, has_side_effects=True, vmem_limit_bytes=VMEM_LIMIT
        ),
        name="exchange",
    )(sec, ref, range_start, azimuth_start, vector, basis, project, own, full)


def final_kernel(back_ref, time_ref, trig_ref, inverse_ref, out_ref, mid_ref):
    def rows(step, _):
        at = pl.ds(pl.multiple_of(step * 192, 192), 192)
        block = split_value(back_ref[pl.ds(step * 8, 8)].reshape(192, KEEP))
        result = dot3(block, (inverse_ref[0], inverse_ref[1]))
        for a in range(3):
            mid_ref[a, at, :] = result[:, a * 128 : (a + 1) * 128]
        return 0

    lax.fori_loop(0, 4, rows, 0)

    def last_chunk(a, _):
        for group in range(2):
            count = 8 if group == 0 else 4
            for n1, (sr, si) in enumerate(dft32(untwist(mid_ref, trig_ref, a, group), 1)):
                re, im = get_pair(time_ref.at[n1 * 3 + a], 0, group)
                at = group * 8 * 192 + (n1 * 3 + a) * 2
                out_ref[pl.ds(at, count, stride=192), :] = (sr * re + si * im)[0:count]
                out_ref[pl.ds(at + 1, count, stride=192), :] = (si * re - sr * im)[0:count]
        return 0

    lax.fori_loop(0, 3, last_chunk, 0)


def final(back, time, trig, inverse):
    return pl.pallas_call(
        final_kernel,
        out_shape=jax.ShapeDtypeStruct((2 * LINES * 96, 128), F32),
        scratch_shapes=[pltpu.VMEM((3, PEERS * ROWS, 128), F32)],
        compiler_params=pltpu.CompilerParams(vmem_limit_bytes=VMEM_LIMIT),
        name="range_final",
    )(back, time, trig, inverse)


def body(reference_slc, secondary_slc, range_start, azimuth_start):
    own, full = (jnp.asarray(t) for t in azimuth_tables())
    basis, inverse, project = (jnp.asarray(t) for t in range_tables())
    sec = secondary_slc.reshape(2, LINES, 96, 128).transpose(1, 2, 0, 3).reshape(2 * LINES * 96, 128)
    ref = reference_slc.transpose(1, 0, 2)
    back, time, trig = exchange(
        sec, ref, range_start, azimuth_start, jnp.asarray(vector_table()), basis, project, own, full
    )
    out = final(back, time, trig, inverse)
    return out.reshape(LINES, 96, 2, 128).transpose(2, 0, 1, 3).reshape(1, 2, LINES, RG)


def solution(mesh):
    in_specs = (P(None, "line", "date"), P("date", None, "line", None), P("date"), P("date"))
    out_specs = P("date", None, "line", None)
    return jax.shard_map(body, mesh=mesh, in_specs=in_specs, out_specs=out_specs, check_vma=False)
```

```python
import math

import jax
import jax.numpy as jnp
import ml_dtypes
import numpy as np
from jax import lax
from jax.experimental import pallas as pl
from jax.experimental.pallas import tpu as pltpu
from jax.sharding import PartitionSpec as P

RG = 12288
AZ = 384
OUTER = 32
INNER = 384
KEEP = 256
LINES = 12
ROWS = 24
PEERS = 32
MESH = pl.DeviceIdType.MESH
F32 = jnp.float32
BF16 = jnp.bfloat16
VMEM_LIMIT = 56 * 1024 * 1024


def row_line():
    return np.array(list(range(8)) + list(range(8)) + list(range(8, 12)) * 2)


def row_part():
    return np.array([0] * 8 + [1] * 8 + [0] * 4 + [1] * 4)


def dirichlet(offset, width, length):
    offset = np.asarray(offset)
    safe = np.where(offset == 0, 1, offset)
    value = np.sin(np.pi * width * safe / length) / (length * np.sin(np.pi * safe / length))
    return np.where(offset == 0, width / length, value)


def split_table(table):
    table = np.asarray(table, np.float32)
    high = table.astype(ml_dtypes.bfloat16)
    low = (table - high.astype(np.float32)).astype(ml_dtypes.bfloat16)
    return np.stack([high, low])


def azimuth_tables():
    lines = (np.arange(PEERS)[:, None] * LINES + row_line()[None]).reshape(-1)
    part = np.tile(row_part(), PEERS)
    full = dirichlet(lines[:, None] - lines[None, :], AZ // 2, AZ)
    own = full * (part[:, None] == part[None, :])
    return split_table(own), full.astype(np.float32).reshape(4, 192, 768)


def range_tables():
    n2 = np.arange(INNER)
    angle = 2 * np.pi * (np.arange(KEEP // 2)[None, :] + 0.5) * n2[:, None] / INNER
    basis = math.sqrt(2 / INNER) * np.concatenate([np.cos(angle), np.sin(angle)], 1)
    projection = dirichlet(n2[:, None] - n2[None, :], KEEP, INNER)
    return split_table(basis), split_table(basis.T / OUTER**2), split_table(projection)


def cmul_const(re, im, angle):
    c, s = math.cos(angle), math.sin(angle)
    if abs(c - 1) < 1e-12:
        return re, im
    if abs(c) < 1e-12:
        return (-im, re) if s > 0 else (im, -re)
    if abs(abs(c) - abs(s)) < 1e-12:
        r = math.sqrt(0.5)
        if c > 0 and s > 0:
            return (re - im) * r, (re + im) * r
        if c > 0:
            return (re + im) * r, (im - re) * r
        if s > 0:
            return (re + im) * -r, (re - im) * r
        return (im - re) * r, (re + im) * -r
    return re * c - im * s, re * s + im * c


def dft_small(values, sign):
    n = len(values)
    if n == 1:
        return values
    even = dft_small(values[0::2], sign)
    odd = dft_small(values[1::2], sign)
    low, high = [], []
    for k in range(n // 2):
        tr, ti = cmul_const(odd[k][0], odd[k][1], sign * 2 * math.pi * k / n)
        low.append((even[k][0] + tr, even[k][1] + ti))
        high.append((even[k][0] - tr, even[k][1] - ti))
    return low + high


def dft32(load, sign):
    middle = []
    for q in range(8):
        part = dft_small([load(q + 8 * p) for p in range(4)], sign)
        middle.append([cmul_const(*part[s], sign * 2 * math.pi * q * s / 32) for s in range(4)])
    out = [None] * 32
    for s in range(4):
        part = dft_small([middle[q][s] for q in range(8)], sign)
        for t in range(8):
            out[s + 4 * t] = part[t]
    return out


def split_value(x):
    high = x.astype(BF16)
    low = (x - high.astype(F32)).astype(BF16)
    return high, low


def dot(a, b):
    return jnp.dot(a, b, preferred_element_type=F32)


def dot3(a, b):
    return dot(a[0], b[0]) + dot(a[1], b[0]) + dot(a[0], b[1])


TWIST, VECTOR, PHASE, TRIG = 0, 192, 208, 240


def vector_table():
    table = np.zeros((2, 16, 128), np.float32)
    lines = (np.arange(PEERS)[:, None] * LINES + row_line()[None]).reshape(6, 128)
    real = np.tile(row_part() == 0, PEERS).reshape(6, 128)
    table[0, 0:6] = lines
    table[0, 8:14] = lines
    table[1, 0:6] = np.where(real, 0, -RG // 4)
    table[1, 8:14] = np.where(real, RG // 4, 0)
    return table


def cosine(turns):
    rest = turns - jnp.floor(turns * (1.0 / RG)) * RG
    half = (rest * (1.0 / RG) - 0.5) * math.pi
    square = half * half
    value = jnp.full_like(square, -1.0 / math.factorial(14))
    for k in range(6, -1, -1):
        value = value * square + (-1) ** k / math.factorial(2 * k)
    return 1 - 2 * value * value


def fill_trig(trig_ref, vector_ref, range_first, azimuth_first, line):
    k1 = lax.broadcasted_iota(jnp.int32, (OUTER, 128), 0)
    lane = lax.broadcasted_iota(jnp.int32, (OUTER, 128), 1)
    bins = (range_first + ((k1 - range_first) & (OUTER - 1)) + OUTER * (KEEP - 1) // 2).astype(F32)
    for a in range(3):
        turns = bins * (lane + a * 128).astype(F32)
        trig_ref[a * OUTER : (a + 1) * OUTER, :] = cosine(turns)
        trig_ref[96 + a * OUTER : 96 + (a + 1) * OUTER, :] = cosine(turns - RG // 4)
    factor = ((RG // (2 * AZ)) * (2 * azimuth_first + AZ // 2 - 1)).astype(F32)
    trig_ref[VECTOR : VECTOR + 16, :] = cosine(vector_ref[0] * factor + vector_ref[1])
    turns = (line * LINES + k1[0:16]).astype(F32) * factor
    trig_ref[PHASE : PHASE + 16, :] = cosine(turns)
    trig_ref[PHASE + 16 : PHASE + 32, :] = cosine(turns - RG // 4)


def remote(src, dst, send, recv, date, line):
    return pltpu.make_async_remote_copy(
        src_ref=src, dst_ref=dst, send_sem=send, recv_sem=recv, device_id=(date, line), device_id_type=MESH
    )


def chunk_of(zh, y):
    skip = 3 - y
    return jnp.where(zh > skip, zh - 1, zh), zh != skip


def get_pair(ref, base, group):
    if group == 0:
        return ref[base : base + 8, :], ref[base + 8 : base + 16, :]
    tile = ref[base + 16 : base + 24, :]
    return tile, pltpu.roll(tile, 4, 0)


def put_pair(ref, base, group, re, im):
    if group == 0:
        ref[base : base + 8, :] = re
        ref[base + 8 : base + 16, :] = im
    else:
        ref[base + 16 : base + 24, :] = jnp.concatenate([re[0:4], im[0:4]], 0)


def untwist(mid, trig_ref, a, group):
    def load(k1):
        c, s = twiddle(trig_ref, a, k1)
        re, im = get_pair(mid.at[a], k1 * ROWS, group)
        return re * c - im * s, im * c + re * s

    return load


def twiddle(trig_ref, a, k1):
    row = a * OUTER + k1
    return trig_ref[pl.ds(row, 1), :], trig_ref[pl.ds(96 + row, 1), :]


STEPS = 8
PIECES = 2
PIECE = 8 * ROWS // PIECES


def exchange_kernel(
    sec_ref, refr_ref, range_ref, azimuth_ref, vector_ref, basis_ref, project_ref, own_hbm, full_hbm,
    back_ref, time_out, trig_out,
    trig_ref, mid_ref, coef_ref, spread_ref, chunks_ref, all_ref, vecs_ref, filt_ref, lines_ref, time_ref, rout_ref,
    own_ref, full_ref, mixed_ref,
    a_send, a_recv, b_send, b_recv, x_send, x_recv, v_send, v_recv, y_send, y_recv,
    r_send, r_recv, l_send, l_recv, own_sem, xo_sem,
):
    d, l = lax.axis_index("date"), lax.axis_index("line")
    x, zh = d // 4, d % 4
    zl, u = l // 8, l % 8
    y = u // 2
    z = zh * 4 + zl
    up, down = (z + 1) % 16, (z + 15) % 16
    right = (x * 4 + up // 4, (up % 4) * 8 + u)
    left = (x * 4 + down // 4, (down % 4) * 8 + u)
    place = x * 8 + u
    mine, valid = chunk_of(zh, y)

    own_copy = pltpu.make_async_copy(own_hbm, own_ref, own_sem.at[4])
    own_copy.start()
    full_copy = pltpu.make_async_copy(full_hbm.at[zl], full_ref, own_sem.at[5])
    full_copy.start()

    def plane(i):
        other = (place + i) % PEERS
        ox, ou = other // 8, other % 8
        return other, ox, ou, ox * 4 + zh, zl * 8 + ou

    barrier = pltpu.get_barrier_semaphore()

    def greet(i, _):
        pl.semaphore_signal(barrier, inc=1, device_id=(d, (l + i) % PEERS), device_id_type=MESH)
        _, _, _, od, ol = plane(i)
        pl.semaphore_signal(barrier, inc=1, device_id=(od, ol), device_id_type=MESH)
        return 0

    pl.semaphore_signal(barrier, inc=1, device_id=right, device_id_type=MESH)
    pl.semaphore_signal(barrier, inc=1, device_id=left, device_id_type=MESH)
    lax.fori_loop(1, PEERS, greet, 0)

    for i in range(LINES):
        for part in range(2):
            row = i + 8 * part if i < 8 else 8 + i + 4 * part
            for c in range(6):
                chunks_ref[c, row : row + 1, :] = refr_ref[i, part : part + 1, c * 128 : (c + 1) * 128]

    fill_trig(trig_ref, vector_ref, range_ref[0], azimuth_ref[0], l)
    trig_out[...] = trig_ref[...]

    pl.semaphore_wait(barrier, 2 * (PEERS - 1) + 2)

    def y_slot(i, source):
        return all_ref.at[i, zl, pl.ds(pl.multiple_of(source * ROWS, 8), ROWS)]

    def y_copy(c):
        q = 6 * zh + c
        return remote(chunks_ref.at[c], y_slot(q // 8, u), y_send.at[c], y_recv.at[u], d, zl * 8 + q % 8)

    def y_own(c):
        return pltpu.make_async_copy(chunks_ref.at[c], y_slot((6 * zh + c) // 8, u), own_sem.at[0])

    for c in range(6):
        owner = (6 * zh + c) % 8

        @pl.when(owner != u)
        def _():
            y_copy(c).start()

        @pl.when(owner == u)
        def _():
            y_own(c).start()

    def v_copy(i, slot):
        return remote(
            trig_ref.at[pl.ds(VECTOR, 16)], vecs_ref.at[slot], v_send.at[i], v_recv.at[slot],
            (x + i) % 4 * 4 + zh, l,
        )

    for i in range(1, 4):
        v_copy(i, x).start()
    own_vec = pltpu.make_async_copy(trig_ref.at[pl.ds(VECTOR, 16)], vecs_ref.at[x], own_sem.at[1])
    own_vec.start()

    def chunk(a, _):
        for group in range(2):
            rows = 8 if group == 0 else 4
            first = 8 * group
            pc = trig_ref[PHASE + first : PHASE + first + rows, :]
            ps = trig_ref[PHASE + 16 + first : PHASE + 16 + first + rows, :]

            def load(n1):
                at = first * 192 + (n1 * 3 + a) * 2
                return sec_ref[pl.ds(at, rows, stride=192), :], sec_ref[pl.ds(at + 1, rows, stride=192), :]

            for k1, (re, im) in enumerate(dft32(load, -1)):
                c, s = twiddle(trig_ref, a, k1)
                re, im = re * c + im * s, im * c - re * s
                re, im = re * pc + im * ps, im * pc - re * ps
                put_pair(mid_ref.at[a], k1 * ROWS, group, re, im)
        return 0

    def ring_copy(origin, send, recv, step, piece, to):
        i, ok = chunk_of(origin // 4, y)
        ref = all_ref.at[jnp.where(ok, i, 0), origin % 4, pl.ds(piece * PIECE, PIECE)]
        at = step * PIECES + piece
        return ok, remote(ref, ref, send.at[at], recv.at[at], *to)

    def ring_start(s, p):
        ok, copy = ring_copy((z + 17 - s) % 16, r_send, r_recv, s, p, right)
        pl.when(ok)(copy.start)
        if s < STEPS:
            ok2, copy2 = ring_copy((z + s - 1) % 16, l_send, l_recv, s, p, left)
            pl.when(ok2)(copy2.start)

    def ring_sent(s, p):
        ok, copy = ring_copy((z + 17 - s) % 16, r_send, r_recv, s, p, right)
        pl.when(ok)(copy.wait_send)
        if s < STEPS:
            ok2, copy2 = ring_copy((z + s - 1) % 16, l_send, l_recv, s, p, left)
            pl.when(ok2)(copy2.wait_send)

    def ring_arrived(s, p):
        ok, copy = ring_copy((z + 16 - s) % 16, r_send, r_recv, s, p, left)
        pl.when(ok)(copy.wait_recv)
        if s < STEPS:
            ok2, copy2 = ring_copy((z + s) % 16, l_send, l_recv, s, p, right)
            pl.when(ok2)(copy2.wait_recv)

    def ring_step(s):
        for p in range(PIECES):
            if s > 1:
                ring_arrived(s - 1, p)
            if s <= STEPS:
                ring_start(s, p)

    def a_copy(to):
        return remote(coef_ref.at[to], spread_ref.at[l], a_send.at[to], a_recv.at[l], d, to)

    def send_blocks(copy, step):
        def send(i, _):
            to = step * 8 + (u + i) % 8
            pl.when(to != l)(copy(to).start)
            return 0

        lax.fori_loop(0, 8, send, 0)

    def rows(k, _):
        step = (zl + k) % 4
        at = pl.ds(pl.multiple_of(step * 192, 192), 192)
        block = jnp.concatenate([mid_ref[a, at, :] for a in range(3)], 1)
        result = dot3(split_value(block), (basis_ref[0], basis_ref[1]))
        coef_ref[pl.ds(step * 8, 8)] = result.reshape(8, ROWS, KEEP)
        return 0

    def cross(k, _):
        send_blocks(a_copy, (zl + k) % 4)
        return 0

    def cross_part(part):
        def send(n, _):
            copy = a_copy((zl + 1 + n // 8) % 4 * 8 + (u + n) % 8)
            copy.start()
            return 0

        lax.fori_loop(3 * part, 3 * part + 3 if part < 5 else 24, send, 0)

    def a_own():
        return pltpu.make_async_copy(coef_ref.at[l], spread_ref.at[l], own_sem.at[2])

    def mix():
        row = lax.broadcasted_iota(jnp.int32, (ROWS, 128), 0)
        real = (row < 8) | ((row >= 16) & (row < 20))
        for i in range(1, 4):
            v_copy(i, (x + i) % 4).wait_recv()
        own_vec.wait()
        full_copy.wait()

        def date(t, _):
            at = pl.ds(pl.multiple_of(t * 8 * ROWS, 8 * ROWS), 8 * ROWS)
            for j in range(6):
                lanes = slice(j * 128, (j + 1) * 128)
                mixed = jnp.where(real, vecs_ref[t, j : j + 1, :], vecs_ref[t, 8 + j : 9 + j, :])
                part = (full_ref[:, lanes].reshape(8, ROWS, 128) * mixed[None]).reshape(8 * ROWS, 128)
                high, low = split_value(part)
                mixed_ref[0, at, lanes] = high
                mixed_ref[1, at, lanes] = low
            return 0

        lax.fori_loop(0, 4, date, 0)

    def x_copy(t, i, ou):
        return remote(
            rout_ref.at[t, i, ou], lines_ref.at[x * 24 + i * 8 + u], x_send.at[(t * 3 + i) * 8 + ou],
            x_recv.at[i * PEERS + place], t * 4 + zh, zl * 8 + ou,
        )

    def x_own(i):
        return pltpu.make_async_copy(rout_ref.at[x, i, u], lines_ref.at[x * 24 + i * 8 + u], xo_sem.at[i])

    def ref_chunk(block):
        i, ok = chunk_of(block % 4, y)

        @pl.when(ok)
        def _():
            samples = split_value(all_ref[i].reshape(2 * AZ, 128))

            def date(k, _):
                t = (x + 1 + k) % 4
                at = pl.ds(pl.multiple_of(t * 8 * ROWS, 8 * ROWS), 8 * ROWS)
                result = dot3((mixed_ref[0, at, :], mixed_ref[1, at, :]), samples)
                rout_ref[t, i] = result.reshape(8, ROWS, 128)

                def send(j, _):
                    ou = (u + j) % 8
                    pl.when((t != x) | (ou != u))(x_copy(t, i, ou).start)
                    return 0

                lax.fori_loop(0, 8, send, 0)
                return 0

            lax.fori_loop(0, 4, date, 0)
            x_own(i).start()

    def b_copy(to):
        return remote(filt_ref.at[to], back_ref.at[l], b_send.at[to], b_recv.at[l], d, to)

    def b_own():
        return pltpu.make_async_copy(filt_ref.at[l], back_ref.at[l], own_sem.at[3])

    def second():
        a_own().wait()
        own_copy.wait()

        def arrived(i, _):
            source = (l + i) % PEERS
            remote(
                coef_ref.at[source], spread_ref.at[source], a_send.at[source], a_recv.at[source], d, source
            ).wait_recv()
            return 0

        lax.fori_loop(1, PEERS, arrived, 0)
        sec = split_value(spread_ref[...].reshape(PEERS * ROWS, KEEP))

        def sec_rows(k, _):
            step = (zl + 1 + k) % 4
            at = pl.ds(pl.multiple_of(step * 192, 192), 192)
            result = dot3((own_ref[0, at, :], own_ref[1, at, :]), sec)
            filt_ref[pl.ds(step * 8, 8)] = result.reshape(8, ROWS, KEEP)
            send_blocks(b_copy, step)
            return 0

        lax.fori_loop(0, 4, sec_rows, 0)
        b_own().start()

    def x_other(k, i):
        other, ox, ou, od, ol = plane(k)
        return remote(
            rout_ref.at[ox, i, ou], lines_ref.at[ox * 24 + i * 8 + ou], x_send.at[(ox * 3 + i) * 8 + ou],
            x_recv.at[i * PEERS + other], od, ol,
        )

    def time_copy():
        return pltpu.make_async_copy(time_ref, time_out, own_sem.at[1])

    def ref_range():
        def arrived(k, _):
            for i in range(3):
                x_other(k, i).wait_recv()
            return 0

        for i in range(3):
            x_own(i).wait()
        lax.fori_loop(1, PEERS, arrived, 0)

        def forward_chunk(a, _):
            for group in range(2):

                def load(n1):
                    return get_pair(lines_ref.at[n1 * 3 + a], 0, group)

                for k1, (re, im) in enumerate(dft32(load, -1)):
                    c, s = twiddle(trig_ref, a, k1)
                    put_pair(mid_ref.at[a], k1 * ROWS, group, re * c + im * s, im * c - re * s)
            return 0

        lax.fori_loop(0, 3, forward_chunk, 0)

        def project_rows(step, _):
            at = pl.ds(pl.multiple_of(step * 192, 192), 192)
            block = jnp.concatenate([mid_ref[a, at, :] for a in range(3)], 1)
            result = dot3(split_value(block), (project_ref[0], project_ref[1]))
            for a in range(3):
                mid_ref[a, at, :] = result[:, a * 128 : (a + 1) * 128]
            return 0

        lax.fori_loop(0, 4, project_rows, 0)

        def time_chunk(a, _):
            for group in range(2):
                for n1, (re, im) in enumerate(dft32(untwist(mid_ref, trig_ref, a, group), 1)):
                    put_pair(time_ref.at[n1 * 3 + a], 0, group, re, im)
            return 0

        lax.fori_loop(0, 3, time_chunk, 0)
        time_copy().start()

    chunk(0, 0)

    @pl.when(valid)
    def _():
        for i in range(1, 8):
            source = (u + i) % 8
            remote(
                chunks_ref.at[0], y_slot(mine, source), y_send.at[0], y_recv.at[source], d, zl * 8 + source
            ).wait_recv()
        y_own(0).wait()

    ring_step(1)
    lax.fori_loop(1, 3, chunk, 0)
    ring_step(2)
    lax.fori_loop(0, 4, rows, 0)
    a_own().start()
    cross(0, 0)
    mix()
    for s in range(3, STEPS + 1):
        ring_step(s)
        if s - 3 < 6:
            cross_part(s - 3)
        if s == 4:
            ref_chunk(zh)
        if s == 6:
            ref_chunk(zh + jnp.where(zl >= 2, 1, 3))
    ref_chunk(zh + jnp.where(zl >= 2, 3, 1))
    ring_step(STEPS + 1)
    ref_chunk(zh + 2)
    second()
    ref_range()
    for s in range(1, STEPS + 1):
        for p in range(PIECES):
            ring_sent(s, p)
    for i in range(1, 4):
        v_copy(i, x).wait_send()
    for c in range(6):
        owner = (6 * zh + c) % 8

        @pl.when(owner != u)
        def _():
            y_copy(c).wait_send()

    def finish(k, _):
        for i in range(3):
            x_other(k, i).wait_send()
        to = (l + k) % PEERS
        a_copy(to).wait_send()
        b_copy(to).wait_send()
        remote(filt_ref.at[to], back_ref.at[to], b_send.at[to], b_recv.at[to], d, to).wait_recv()
        return 0

    lax.fori_loop(1, PEERS, finish, 0)
    b_own().wait()
    time_copy().wait()


def exchange(sec, ref, range_start, azimuth_start, vector, basis, project, own, full):
    any_space = pl.BlockSpec(memory_space=pl.ANY)
    vmem = pl.BlockSpec(memory_space=pltpu.VMEM)
    smem = pl.BlockSpec(memory_space=pltpu.SMEM)
    dma = pltpu.SemaphoreType.DMA
    blocks = (PEERS, ROWS, KEEP)
    time = (96, ROWS, 128)
    peers = dma((PEERS,))
    ring = dma(((STEPS + 1) * PIECES,))
    return pl.pallas_call(
        exchange_kernel,
        out_shape=(
            jax.ShapeDtypeStruct(blocks, F32),
            jax.ShapeDtypeStruct(time, F32),
            jax.ShapeDtypeStruct((TRIG, 128), F32),
        ),
        in_specs=[vmem, vmem, smem, smem, vmem, vmem, vmem, any_space, any_space],
        out_specs=(any_space, any_space, vmem),
        scratch_shapes=[
            pltpu.VMEM((TRIG, 128), F32),
            pltpu.VMEM((3, PEERS * ROWS, 128), F32),
            pltpu.VMEM(blocks, F32),
            pltpu.VMEM(blocks, F32),
            pltpu.VMEM((6, ROWS, 128), F32),
            pltpu.VMEM((3, 4, 8 * ROWS, 128), F32),
            pltpu.VMEM((4, 16, 128), F32),
            pltpu.VMEM(blocks, F32),
            pltpu.VMEM(time, F32),
            pltpu.VMEM(time, F32),
            pltpu.VMEM((4, 3, 8, ROWS, 128), F32),
            pltpu.VMEM((2, 2 * AZ, 2 * AZ), BF16),
            pltpu.VMEM((8 * ROWS, 2 * AZ), F32),
            pltpu.VMEM((2, 2 * AZ, 2 * AZ), BF16),
            peers, peers, peers, peers, dma((3 * PEERS,)), dma((3 * PEERS,)),
            dma((4,)), dma((4,)), dma((6,)), dma((8,)),
            ring, ring, ring, ring, dma((6,)), dma((3,)),
        ],
        compiler_params=pltpu.CompilerParams(
            collective_id=1, has_side_effects=True, vmem_limit_bytes=VMEM_LIMIT
        ),
        name="exchange",
    )(sec, ref, range_start, azimuth_start, vector, basis, project, own, full)


def final_kernel(back_ref, time_ref, trig_ref, inverse_ref, out_ref, mid_ref):
    def rows(step, _):
        at = pl.ds(pl.multiple_of(step * 192, 192), 192)
        block = split_value(back_ref[pl.ds(step * 8, 8)].reshape(192, KEEP))
        result = dot3(block, (inverse_ref[0], inverse_ref[1]))
        for a in range(3):
            mid_ref[a, at, :] = result[:, a * 128 : (a + 1) * 128]
        return 0

    lax.fori_loop(0, 4, rows, 0)

    def last_chunk(a, _):
        for group in range(2):
            count = 8 if group == 0 else 4
            for n1, (sr, si) in enumerate(dft32(untwist(mid_ref, trig_ref, a, group), 1)):
                re, im = get_pair(time_ref.at[n1 * 3 + a], 0, group)
                at = group * 8 * 192 + (n1 * 3 + a) * 2
                out_ref[pl.ds(at, count, stride=192), :] = (sr * re + si * im)[0:count]
                out_ref[pl.ds(at + 1, count, stride=192), :] = (si * re - sr * im)[0:count]
        return 0

    lax.fori_loop(0, 3, last_chunk, 0)


def final(back, time, trig, inverse):
    return pl.pallas_call(
        final_kernel,
        out_shape=jax.ShapeDtypeStruct((2 * LINES * 96, 128), F32),
        scratch_shapes=[pltpu.VMEM((3, PEERS * ROWS, 128), F32)],
        compiler_params=pltpu.CompilerParams(vmem_limit_bytes=VMEM_LIMIT),
        name="range_final",
    )(back, time, trig, inverse)


def body(reference_slc, secondary_slc, range_start, azimuth_start):
    own, full = (jnp.asarray(t) for t in azimuth_tables())
    basis, inverse, project = (jnp.asarray(t) for t in range_tables())
    sec = secondary_slc.reshape(2, LINES, 96, 128).transpose(1, 2, 0, 3).reshape(2 * LINES * 96, 128)
    ref = reference_slc.transpose(1, 0, 2)
    back, time, trig = exchange(
        sec, ref, range_start, azimuth_start, jnp.asarray(vector_table()), basis, project, own, full
    )
    out = final(back, time, trig, inverse)
    return out.reshape(LINES, 96, 2, 128).transpose(2, 0, 1, 3).reshape(1, 2, LINES, RG)


def solution(mesh):
    in_specs = (P(None, "line", "date"), P("date", None, "line", None), P("date"), P("date"))
    out_specs = P("date", None, "line", None)
    return jax.shard_map(body, mesh=mesh, in_specs=in_specs, out_specs=out_specs, check_vma=False)
```
